512 devices in a mesh: fibre: 128 (over y_lo, z, x), win: 4 (over y_hi, core).
Axes of the slice: x: 4, y: 4 (y_hi: 2, y_lo: 2; y = y_hi * 2 + y_lo), z: 16, core: 2. Of those that a mesh axis runs over, the one named last changes fastest.
Arguments:
- samples_data: bfloat16 [8, 2000, 32768], P('win', None, 'fibre'), may hold values from -6 to 6
- coupling: float32 [32768], P('fibre'), may hold values from 0.1 to 1
Outputs:
- dispersion: float32 [8192, 400], P('fibre', 'win')
The draws below stay inside these ranges and needn't reach their ends.
All inputs are finite; a program needn't handle non-finite values.
Results may differ from the reference program's by a relative error of at most 0.0031.
Values may be sent and summed in bfloat16 or wider, within the bound.
No kernel may reach another device: no remote copies, remote signals or barrier semaphores. Data moves between devices by JAX's collectives and lax.ppermute only.
A program may use at most 64 MiB of HBM per device.

```python
import math
import jax
import jax.numpy as jnp
from jax import lax

SAMPLES = 2000
FREQS = 400
OFFS = 256
VEL = 512
SEG_BLOCKS = 8
WINDOWS = 8
CHANNELS = 32768
SEGMENTS = 16


def levels(stream_key, extent, cuts, low, high):
    gain, own = 1.0, jax.random.fold_in(stream_key, 6)
    for dim, shards_of in cuts:
        draws = jnp.exp(jax.random.uniform(jax.random.fold_in(own, dim), (shards_of,), jnp.float32, low / len(cuts), high / len(cuts)))
        gain = gain * jnp.repeat(draws, extent[dim] // shards_of).reshape([-1 if axis == dim else 1 for axis in range(len(extent))])
    return gain


def noise(rng, dims, scale, limit, shards=(), kind=jnp.bfloat16):
    entries = scale * jax.random.normal(rng, dims, jnp.float32)
    if shards:
        entries = entries * levels(rng, dims, shards, -0.22, 0.18)
    return jnp.clip(entries, -limit, limit).astype(kind)


def setup_inputs(seed: int = 0) -> dict:
    splits = jax.random.split(jax.random.key(seed), 3)
    samples_data = noise(splits[0], (WINDOWS, SAMPLES, CHANNELS), 1.0, 6.0, ((0, 4), (2, 128)))
    coupling = jnp.clip(jnp.exp(math.log(1.0) - 2.3025851 * jax.random.uniform(splits[1], (CHANNELS,), jnp.float32) ** levels(splits[1], (CHANNELS,), ((0, 128),), -0.2, 0.2)), 0.1, 1.0)
    return {"samples_data": samples_data, "coupling": coupling}


EPS = 1e-06

def time_table(samples, freqs):
    times = jnp.arange(samples, dtype=jnp.int32)
    bins = jnp.arange(freqs, dtype=jnp.int32) + 1
    phase_int = bins[:, None] * times[None, :] % samples
    angle = 2.0 * math.pi / samples * phase_int.astype(jnp.float32)
    return jnp.concatenate([jnp.cos(angle), jnp.sin(angle)], axis=0).astype(jnp.bfloat16)

def whiten(block, weights, table):
    freqs = table.shape[0] // 2
    raw = jnp.einsum('gt,wtc->wgc', table.astype(jnp.float32), block.astype(jnp.float32), precision=lax.Precision.HIGHEST)
    real_part = raw[:, :freqs]
    imag_part = -raw[:, freqs:]
    power = lax.optimization_barrier(jnp.mean(real_part * real_part + imag_part * imag_part, axis=1, keepdims=True))
    factor = weights[None, None, :] / jnp.sqrt(power + EPS)
    return jnp.concatenate([real_part * factor, imag_part * factor], axis=2).astype(jnp.bfloat16)

def phase_image(stack, bin_index, speed_index, width):
    real_part = stack[:, :width]
    imag_part = stack[:, width:]
    power = lax.optimization_barrier(jnp.mean(real_part * real_part + imag_part * imag_part, axis=1, keepdims=True))
    factor = 1.0 / jnp.sqrt(power + EPS)
    real_part = (real_part * factor).astype(jnp.bfloat16).astype(jnp.float32)
    imag_part = (imag_part * factor).astype(jnp.bfloat16).astype(jnp.float32)
    lags = jnp.arange(width, dtype=jnp.int32)
    cycles = ((bin_index[:, None] + 1) * lags[None, :]).astype(jnp.float32)
    speed = 150.0 + 1350.0 * speed_index.astype(jnp.float32) / (VEL - 1)
    turns = cycles[:, :, None] * (200.0 * 8.0 / SAMPLES / speed)[None, None, :]
    angle = 2.0 * math.pi * (turns - jnp.floor(turns))
    cosines = jnp.cos(angle).astype(jnp.bfloat16).astype(jnp.float32)
    sines = jnp.sin(angle).astype(jnp.bfloat16).astype(jnp.float32)
    highest = lax.Precision.HIGHEST
    along = jnp.einsum('fk,fkv->fv', real_part, cosines, precision=highest) + jnp.einsum('fk,fkv->fv', imag_part, sines, precision=highest)
    across = jnp.einsum('fk,fkv->fv', imag_part, cosines, precision=highest) - jnp.einsum('fk,fkv->fv', real_part, sines, precision=highest)
    return ((along * along + across * across) / width).T

def correlate(pair):
    here, after = pair
    width = here.shape[2] // 2
    xval = here.astype(jnp.float32)
    zval = after.astype(jnp.float32)
    xcomp = xval[..., :width] + 1j * xval[..., width:]
    zcomp = zval[..., :width] + 1j * zval[..., width:]
    first = jnp.fft.fft(xcomp, n=2 * width, axis=-1)
    second = jnp.fft.fft(jnp.concatenate([xcomp, zcomp], axis=-1), axis=-1)
    summed = lax.optimization_barrier(jnp.sum(first * jnp.conj(second), axis=0))
    lagged = jnp.fft.fft(summed, axis=-1)[:, :width] / (2 * width)
    return jnp.concatenate([jnp.real(lagged), jnp.imag(lagged)], axis=-1).astype(jnp.float32)

def reference(samples_data, coupling):
    blocks_count = CHANNELS // OFFS
    table = time_table(SAMPLES, FREQS)
    blocks = jnp.moveaxis(samples_data.reshape(WINDOWS, SAMPLES, blocks_count, OFFS), 2, 0)
    weights = coupling.reshape(blocks_count, OFFS)
    whitened = lax.map(lambda pair: whiten(pair[0], pair[1], table), (blocks, weights))
    following = jnp.concatenate([whitened[1:], jnp.zeros_like(whitened[:1])], axis=0)
    stacks = lax.map(correlate, (whitened, following))
    segstack = lax.optimization_barrier(jnp.sum(stacks.reshape(SEGMENTS, SEG_BLOCKS, FREQS, 2 * OFFS), axis=1))
    bins = jnp.arange(FREQS, dtype=jnp.int32)
    speeds = jnp.arange(VEL, dtype=jnp.int32)
    images = lax.map(lambda stack: phase_image(stack, bins, speeds, OFFS), segstack)
    return images.reshape(SEGMENTS * VEL, FREQS)
```

```python
import math

import jax
import jax.numpy as jnp
import ml_dtypes
import numpy as np
from jax import lax
from jax.experimental import pallas as pl
from jax.experimental.pallas import tpu as pltpu
from jax.sharding import Mesh, PartitionSpec as P

SAMPLES = 2000
FREQS = 400
OFFS = 256
VEL = 512
SEG_BLOCKS = 8
EPS = 1e-06

WIN_DEVICES = 4
DESTS = SEG_BLOCKS * WIN_DEVICES
CHUNK = FREQS // WIN_DEVICES
TAKEN = -(-CHUNK // SEG_BLOCKS)
SLOT = 16
LOCAL_WINDOWS = 2
DIGIT = 16
BF16 = jnp.bfloat16
F32 = jnp.float32


def bins_of(block, window_device):
    rows = np.arange(SLOT)
    within = TAKEN * block + rows
    valid = (rows < TAKEN) & (within < CHUNK)
    return np.where(valid, window_device * CHUNK + within, -1)


def time_table():
    bins = np.concatenate([bins_of(d // WIN_DEVICES, d % WIN_DEVICES) for d in range(DESTS)])
    times = np.arange(SAMPLES, dtype=np.int64)
    turns = ((bins[:, None] + 1) * times[None, :]) % SAMPLES
    angle = np.float32(2.0 * math.pi / SAMPLES) * turns.astype(np.float32)
    valid = (bins >= 0)[:, None]
    cosines = np.where(valid, np.cos(angle), 0.0).reshape(DESTS, 1, SLOT, SAMPLES)
    sines = np.where(valid, -np.sin(angle), 0.0).reshape(DESTS, 1, SLOT, SAMPLES)
    both = np.concatenate([cosines, sines], axis=1)
    return both.reshape(DESTS * 2 * SLOT, SAMPLES).astype(np.float32).astype(ml_dtypes.bfloat16)


def wave_order():
    return np.concatenate([np.arange(0, 2 * OFFS, 2), np.arange(1, 2 * OFFS, 2)])


def forward_table():
    rows = np.arange(OFFS)
    angle = 2.0 * np.pi / (2 * OFFS) * ((rows[:, None] * wave_order()[None, :]) % (2 * OFFS))
    cosines, sines = np.cos(angle), np.sin(angle)
    upper = np.concatenate([cosines, -sines], axis=1)
    lower = np.concatenate([sines, cosines], axis=1)
    return np.concatenate([upper, lower], axis=0).astype(np.float32).astype(ml_dtypes.bfloat16)


def inverse_tables():
    lags = np.arange(OFFS)
    angle = 2.0 * np.pi / (2 * OFFS) * ((wave_order()[:, None] * lags[None, :]) % (2 * OFFS))
    cosines, sines = np.cos(angle), np.sin(angle)
    upper = np.concatenate([cosines, -sines], axis=1)
    lower = np.concatenate([sines, cosines], axis=1)
    full = (np.concatenate([upper, lower], axis=0) / (2 * OFFS)).astype(np.float32)
    leading = full.astype(ml_dtypes.bfloat16)
    trailing = (full - leading.astype(np.float32)).astype(ml_dtypes.bfloat16)
    return leading, trailing


def spread_table():
    index = np.arange(OFFS)
    same = (index[:, None] % DIGIT) == (index[None, :] % DIGIT)
    return same.astype(ml_dtypes.bfloat16)


def gather_table():
    table = np.zeros((SEG_BLOCKS * SLOT, CHUNK), np.float32)
    for block in range(SEG_BLOCKS):
        for row in range(TAKEN):
            if TAKEN * block + row < CHUNK:
                table[block * SLOT + row, TAKEN * block + row] = 1.0
    return table


def turn_waves(turns):
    rest = turns - jnp.round(turns)
    half = rest * math.pi
    square = half * half
    sine = half * (
        1.0
        + square
        * (
            -1.0 / 6
            + square
            * (1.0 / 120 + square * (-1.0 / 5040 + square * (1.0 / 362880 - square / 39916800)))
        )
    )
    cosine = 1.0 + square * (
        -0.5
        + square
        * (
            1.0 / 24
            + square
            * (
                -1.0 / 720
                + square * (1.0 / 40320 + square * (-1.0 / 3628800 + square / 479001600))
            )
        )
    )
    return 1.0 - 2.0 * sine * sine, 2.0 * sine * cosine


def basis_tables(block, window_device):
    speeds = jnp.arange(VEL, dtype=jnp.int32)
    speed = 150.0 + 1350.0 * speeds.astype(F32) / (VEL - 1)
    slowness = (200.0 * 8.0 / SAMPLES / speed)[None, :]
    first = window_device * CHUNK + TAKEN * block + 1
    index = jnp.arange(SLOT * DIGIT, dtype=jnp.int32)
    fine = ((first + index // DIGIT) * (index % DIGIT)).astype(F32)[:, None]
    coarse = ((first + index % SLOT) * (index // SLOT * DIGIT)).astype(F32)[:, None]
    fine_cos, fine_sin = turn_waves(fine * slowness)
    coarse_cos, coarse_sin = turn_waves(coarse * slowness)
    fine_table = jnp.concatenate([fine_cos, fine_sin], axis=1).astype(BF16)
    coarse_table = jnp.concatenate([coarse_cos, coarse_sin], axis=1)
    return fine_table, coarse_table


WHITEN_STEPS = 8


def whiten_kernel(samples_ref, table_ref, weights_ref, out_ref, raw_ref, power_ref):
    step = pl.program_id(0)
    rows = table_ref.shape[0]
    table = table_ref[...]

    @pl.when(step == 0)
    def _():
        power_ref[...] = jnp.zeros_like(power_ref)

    for w in range(LOCAL_WINDOWS):
        raw = jnp.dot(table, samples_ref[w], preferred_element_type=F32)
        raw_ref[pl.ds(pl.multiple_of(step * rows, rows), rows), w * OFFS : (w + 1) * OFFS] = raw
        power_ref[w] += jnp.sum((raw * raw).reshape(rows // 8, 8, OFFS), axis=0)

    @pl.when(step == WHITEN_STEPS - 1)
    def _():
        for w in range(LOCAL_WINDOWS):
            power = jnp.sum(power_ref[w], axis=0, keepdims=True) / FREQS
            factor = weights_ref[...] / jnp.sqrt(power + EPS)

            def body(d, carry, w=w, factor=factor):
                for part in range(2):
                    start = pl.multiple_of(d * 2 * SLOT + part * SLOT, SLOT)
                    values = raw_ref[pl.ds(start, SLOT), w * OFFS : (w + 1) * OFFS]
                    lane = (2 * w + part) * OFFS
                    out_ref[d, :, lane : lane + OFFS] = (values * factor).astype(BF16)
                return carry

            lax.fori_loop(0, DESTS, body, 0, unroll=4)


def whiten(samples, weights, table):
    rows = table.shape[0] // WHITEN_STEPS
    return pl.pallas_call(
        whiten_kernel,
        grid=(WHITEN_STEPS,),
        in_specs=[
            pl.BlockSpec((LOCAL_WINDOWS, SAMPLES, OFFS), lambda i: (0, 0, 0)),
            pl.BlockSpec((rows, SAMPLES), lambda i: (i, 0)),
            pl.BlockSpec((1, OFFS), lambda i: (0, 0)),
        ],
        out_specs=pl.BlockSpec((DESTS, SLOT, 4 * OFFS), lambda i: (0, 0, 0)),
        out_shape=jax.ShapeDtypeStruct((DESTS, SLOT, 4 * OFFS), BF16),
        scratch_shapes=[
            pltpu.VMEM((table.shape[0], LOCAL_WINDOWS * OFFS), F32),
            pltpu.VMEM((LOCAL_WINDOWS, 8, OFFS), F32),
        ],
        compiler_params=pltpu.CompilerParams(vmem_limit_bytes=40 << 20),
        cost_estimate=pl.CostEstimate(
            flops=2 * table.shape[0] * SAMPLES * 512, bytes_accessed=7 << 20, transcendentals=0
        ),
        name="whiten",
    )(samples, table, weights)


GROUP = WIN_DEVICES * SLOT
WAVES = 2 * OFFS


def own_kernel(recv_ref, table_ref, last_ref, cross_ref, waves_ref):
    table = table_ref[...]
    for w in range(LOCAL_WINDOWS):
        spectra = recv_ref[:, :, w * WAVES : (w + 1) * WAVES].reshape(DESTS * SLOT, WAVES)
        waves_ref[w] = jnp.dot(spectra, table, preferred_element_type=F32)
        last_ref[w] = waves_ref[w, (SEG_BLOCKS - 1) * GROUP : SEG_BLOCKS * GROUP, :]
    for half in range(2):
        real_at = half * OFFS
        imag_at = WAVES + half * OFFS

        def body(step, total, real_at=real_at, imag_at=imag_at, half=half):
            w = step // WIN_DEVICES
            row = pl.multiple_of(step % WIN_DEVICES * SLOT, SLOT)
            total_real, total_imag = total
            own_real = waves_ref[w, pl.ds(row, SLOT), real_at : real_at + OFFS]
            own_imag = waves_ref[w, pl.ds(row, SLOT), imag_at : imag_at + OFFS]
            for block in range(SEG_BLOCKS):
                if block == SEG_BLOCKS - 1:
                    total_real = total_real + (own_real * own_real + own_imag * own_imag)
                    continue
                at = row + (block + 1) * GROUP
                next_real = waves_ref[w, pl.ds(at, SLOT), real_at : real_at + OFFS]
                next_imag = waves_ref[w, pl.ds(at, SLOT), imag_at : imag_at + OFFS]
                if half == 0:
                    ext_real, ext_imag = own_real + next_real, own_imag + next_imag
                else:
                    ext_real, ext_imag = own_real - next_real, own_imag - next_imag
                total_real = total_real + (own_real * ext_real + own_imag * ext_imag)
                total_imag = total_imag + (own_imag * ext_real - own_real * ext_imag)
                own_real, own_imag = next_real, next_imag
            return total_real, total_imag

        zero = jnp.zeros((SLOT, OFFS), F32)
        total = lax.fori_loop(0, LOCAL_WINDOWS * WIN_DEVICES, body, (zero, zero))
        cross_ref[:, real_at : real_at + OFFS] = total[0]
        cross_ref[:, imag_at : imag_at + OFFS] = total[1]


def own_products(received, table):
    return pl.pallas_call(
        own_kernel,
        out_shape=(
            jax.ShapeDtypeStruct((LOCAL_WINDOWS, GROUP, 2 * WAVES), F32),
            jax.ShapeDtypeStruct((SLOT, 2 * WAVES), F32),
        ),
        in_specs=[pl.BlockSpec(memory_space=pltpu.VMEM)] * 2,
        out_specs=(pl.BlockSpec(memory_space=pltpu.VMEM),) * 2,
        scratch_shapes=[pltpu.VMEM((LOCAL_WINDOWS, DESTS * SLOT, 2 * WAVES), F32)],
        compiler_params=pltpu.CompilerParams(vmem_limit_bytes=40 << 20),
        cost_estimate=pl.CostEstimate(
            flops=2 * 1024 * 512 * 1024, bytes_accessed=8 << 20, transcendentals=0
        ),
        name="own_products",
    )(received, table)


def image_kernel(
    halo_ref,
    table_ref,
    last_ref,
    cross_ref,
    lead_ref,
    trail_ref,
    spread_ref,
    fine_ref,
    coarse_ref,
    out_ref,
):
    table = table_ref[...]
    totals = [
        cross_ref[:, at * OFFS : (at + 1) * OFFS] for at in range(4)
    ]
    for w in range(LOCAL_WINDOWS):
        spectra = halo_ref[:, :, w * WAVES : (w + 1) * WAVES].reshape(GROUP, WAVES)
        waves = jnp.dot(spectra, table, preferred_element_type=F32)
        for half in range(2):
            real_at = half * OFFS
            imag_at = WAVES + half * OFFS
            next_real = waves[:, real_at : real_at + OFFS]
            next_imag = waves[:, imag_at : imag_at + OFFS]
            own_real = last_ref[w, :, real_at : real_at + OFFS]
            own_imag = last_ref[w, :, imag_at : imag_at + OFFS]
            more_real = own_real * next_real + own_imag * next_imag
            more_imag = own_imag * next_real - own_real * next_imag
            more_real = jnp.sum(more_real.reshape(WIN_DEVICES, SLOT, OFFS), axis=0)
            more_imag = jnp.sum(more_imag.reshape(WIN_DEVICES, SLOT, OFFS), axis=0)
            sign = 1.0 if half == 0 else -1.0
            totals[half] = totals[half] + sign * more_real
            totals[2 + half] = totals[2 + half] + sign * more_imag
    cross = jnp.concatenate(totals, axis=1)
    upper = cross.astype(BF16)
    lower = (cross - upper.astype(F32)).astype(BF16)
    both = jnp.concatenate([upper, lower], axis=0)
    stack = jnp.dot(both, lead_ref[...], preferred_element_type=F32)
    stack = stack[:SLOT] + stack[SLOT:]
    stack = stack + jnp.dot(upper, trail_ref[...], preferred_element_type=F32)
    real = stack[:, :OFFS]
    imag = stack[:, OFFS:]
    power = jnp.sum(real * real + imag * imag, axis=1, keepdims=True) / OFFS
    factor = 1.0 / jnp.sqrt(power + EPS)
    size = SLOT * DIGIT
    row = lax.broadcasted_iota(jnp.int32, (size, OFFS), 0)
    lane = lax.broadcasted_iota(jnp.int32, (size, OFFS), 1)
    same_digit = row // SLOT == lane // DIGIT
    same_bin = row % SLOT == lane // DIGIT

    def spread(values):
        normed = values * factor
        repeated = jnp.broadcast_to(normed[None], (DIGIT, SLOT, OFFS)).reshape(size, OFFS)
        picked = jnp.where(same_digit, repeated, 0.0).astype(BF16)
        moved = jnp.dot(picked, spread_ref[...], preferred_element_type=F32)
        return jnp.where(same_bin, moved, 0.0).astype(BF16)

    fine = fine_ref[...]
    of_real = jnp.dot(spread(real), fine, preferred_element_type=F32)
    of_imag = jnp.dot(spread(imag), fine, preferred_element_type=F32)
    part_real = of_real[:, :VEL] + of_imag[:, VEL:]
    part_imag = of_imag[:, :VEL] - of_real[:, VEL:]
    coarse_cos = coarse_ref[:, :VEL]
    coarse_sin = coarse_ref[:, VEL:]
    along = part_real * coarse_cos + part_imag * coarse_sin
    across = part_imag * coarse_cos - part_real * coarse_sin
    along = jnp.sum(along.reshape(DIGIT, SLOT, VEL), axis=0)
    across = jnp.sum(across.reshape(DIGIT, SLOT, VEL), axis=0)
    image = (along * along + across * across) / OFFS
    here = VEL // SEG_BLOCKS
    for block in range(SEG_BLOCKS):
        out_ref[block] = image[:, block * here : (block + 1) * here]


def image_of(halo, table, last, cross, lead, trail, spread, fine, coarse):
    return pl.pallas_call(
        image_kernel,
        out_shape=jax.ShapeDtypeStruct((SEG_BLOCKS, SLOT, VEL // SEG_BLOCKS), F32),
        in_specs=[pl.BlockSpec(memory_space=pltpu.VMEM)] * 9,
        out_specs=pl.BlockSpec(memory_space=pltpu.VMEM),
        compiler_params=pltpu.CompilerParams(vmem_limit_bytes=40 << 20),
        cost_estimate=pl.CostEstimate(
            flops=2 * 700 * 512 * 1024, bytes_accessed=6 << 20, transcendentals=0
        ),
        name="image",
    )(halo, table, last, cross, lead, trail, spread, fine, coarse)


def local(samples_data, coupling):
    whitened = whiten(samples_data, coupling[None, :], jnp.asarray(time_table()))
    received = lax.all_to_all(whitened, ("blk", "win"), 0, 0, tiled=True)
    segments = lax.axis_size("seg")
    first_block = received[:WIN_DEVICES]
    halo = lax.ppermute(first_block, "seg", [(s, s - 1) for s in range(1, segments)])
    table = jnp.asarray(forward_table())
    last, cross = own_products(received, table)
    lead, trail = inverse_tables()
    fine, coarse = basis_tables(lax.axis_index("blk"), lax.axis_index("win"))
    parts = image_of(
        halo,
        table,
        last,
        cross,
        jnp.asarray(lead),
        jnp.asarray(trail),
        jnp.asarray(spread_table()),
        fine,
        coarse,
    )
    parts = lax.all_to_all(parts, "blk", 0, 0, tiled=True)
    return lax.dot_general(
        parts.reshape(SEG_BLOCKS * SLOT, VEL // SEG_BLOCKS),
        jnp.asarray(gather_table()),
        (((0,), (0,)), ((), ())),
        precision=lax.Precision.HIGHEST,
        preferred_element_type=F32,
    )


def solution(mesh):
    segments = mesh.shape["fibre"] // SEG_BLOCKS
    inner = Mesh(
        mesh.devices.reshape(segments, SEG_BLOCKS, mesh.shape["win"]), ("seg", "blk", "win")
    )
    placed = (P("win", None, ("seg", "blk")), P(("seg", "blk")))
    return jax.shard_map(
        local, mesh=inner, in_specs=placed, out_specs=P(("seg", "blk"), "win"), check_vma=False
    )
```

```python
import math

import jax
import jax.numpy as jnp
import ml_dtypes
import numpy as np
from jax import lax
from jax.experimental import pallas as pl
from jax.experimental.pallas import tpu as pltpu
from jax.sharding import Mesh, PartitionSpec as P

SAMPLES = 2000
FREQS = 400
OFFS = 256
VEL = 512
SEG_BLOCKS = 8
EPS = 1e-06

WIN_DEVICES = 4
DESTS = SEG_BLOCKS * WIN_DEVICES
CHUNK = FREQS // WIN_DEVICES
FIRST_BIN = [0, 12, 26, 38, 50, 62, 76, 88, CHUNK]
SLOT = 16
TILE = 8
SENT = 7 * TILE
TAKEN = 4 * TILE
LOCAL_WINDOWS = 2
DIGIT = 16
ROWS = DESTS // 2 * SENT
STEP = 256
STEPS = 4
HALF = SAMPLES // 2
LANES = 128
BF16 = jnp.bfloat16
F32 = jnp.float32


def bins_of(block, window_device):
    rows = np.arange(SLOT)
    within = FIRST_BIN[block] + rows
    return np.where(within < FIRST_BIN[block + 1], window_device * CHUNK + within, -1)


def table_rows():
    bins, parts = [], []
    for pair in range(DESTS // 2):
        dests = [bins_of(d // WIN_DEVICES, d % WIN_DEVICES) for d in (2 * pair, 2 * pair + 1)]
        own = []
        for dest in dests:
            own.append(
                [(dest[r], 0) for r in range(8)]
                + [(dest[r], 1) for r in range(8)]
                + [(dest[r], 0) for r in range(8, 12)]
                + [(dest[r], 1) for r in range(8, 12)]
            )
        mixed = [(dest[r], part) for part in (0, 1) for dest in dests for r in (12, 13)]
        for at, part in own[0] + mixed + own[1]:
            bins.append(at)
            parts.append(part)
    return np.array(bins), np.array(parts)


def time_table():
    bins, parts = table_rows()
    times = np.arange(STEP * STEPS, dtype=np.int64)
    turns = ((bins[:, None] + 1) * times[None, :]) % SAMPLES
    angle = np.float32(2.0 * math.pi / SAMPLES) * turns.astype(np.float32)
    valid = (bins >= 0)[:, None] & (times < SAMPLES // 2)[None, :]
    waves = np.where(parts[:, None] == 0, np.cos(angle), -np.sin(angle))
    table = np.where(valid, waves, 0.0).reshape(ROWS, STEPS, STEP)
    return table.transpose(1, 0, 2).astype(np.float32).astype(ml_dtypes.bfloat16)


def wave_order():
    return np.concatenate([np.arange(0, 2 * OFFS, 2), np.arange(1, 2 * OFFS, 2)])


def forward_table():
    rows = np.arange(OFFS)
    angle = 2.0 * np.pi / (2 * OFFS) * ((rows[:, None] * wave_order()[None, :]) % (2 * OFFS))
    cosines, sines = np.cos(angle), np.sin(angle)
    upper = np.concatenate([cosines, -sines], axis=1)
    lower = np.concatenate([sines, cosines], axis=1)
    return np.concatenate([upper, lower], axis=0).astype(np.float32).astype(ml_dtypes.bfloat16)


def inverse_table():
    lags = np.arange(OFFS)
    angle = 2.0 * np.pi / (2 * OFFS) * ((wave_order()[:, None] * lags[None, :]) % (2 * OFFS))
    cosines, sines = np.cos(angle), np.sin(angle)
    upper = np.concatenate([cosines, -sines], axis=1)
    lower = np.concatenate([sines, cosines], axis=1)
    full = (np.concatenate([upper, lower], axis=0) / (2 * OFFS)).astype(np.float32)
    return full.astype(ml_dtypes.bfloat16)


def spread_table():
    index = np.arange(OFFS)
    same = (index[:, None] % DIGIT) == (index[None, :] % DIGIT)
    return same.astype(ml_dtypes.bfloat16)


def gather_table():
    table = np.zeros((SEG_BLOCKS * SLOT, CHUNK), np.float32)
    for block in range(SEG_BLOCKS):
        for row in range(FIRST_BIN[block + 1] - FIRST_BIN[block]):
            table[block * SLOT + row, FIRST_BIN[block] + row] = 1.0
    return table


def turn_waves(turns):
    rest = turns - jnp.round(turns)
    half = rest * math.pi
    square = half * half
    sine = half * (
        1.0
        + square
        * (
            -1.0 / 6
            + square
            * (1.0 / 120 + square * (-1.0 / 5040 + square * (1.0 / 362880 - square / 39916800)))
        )
    )
    cosine = 1.0 + square * (
        -0.5
        + square
        * (
            1.0 / 24
            + square
            * (
                -1.0 / 720
                + square * (1.0 / 40320 + square * (-1.0 / 3628800 + square / 479001600))
            )
        )
    )
    return 1.0 - 2.0 * sine * sine, 2.0 * sine * cosine


def basis_tables(block, window_device):
    speeds = jnp.arange(VEL, dtype=jnp.int32)
    speed = 150.0 + 1350.0 * speeds.astype(F32) / (VEL - 1)
    slowness = (200.0 * 8.0 / SAMPLES / speed)[None, :]
    first = window_device * CHUNK + (25 * block + 2) // 4 * 2 + 1
    index = jnp.arange(SLOT * DIGIT, dtype=jnp.int32)
    fine = ((first + index // DIGIT) * (index % DIGIT)).astype(F32)[:, None]
    coarse = ((first + index % SLOT) * (index // SLOT * DIGIT)).astype(F32)[:, None]
    fine_cos, fine_sin = turn_waves(fine * slowness)
    coarse_cos, coarse_sin = turn_waves(coarse * slowness)
    fine_table = jnp.concatenate([fine_cos, fine_sin], axis=1).astype(BF16)
    coarse_table = jnp.concatenate([coarse_cos, coarse_sin], axis=1)
    return fine_table, coarse_table


def whiten_kernel(
    samples_hbm,
    table_hbm,
    weights_hbm,
    out_hbm,
    early_ref,
    late_ref,
    table_ref,
    weights_ref,
    raw_ref,
    out_ref,
    in_sems,
    out_sems,
):
    weights_copy = pltpu.make_async_copy(weights_hbm, weights_ref, in_sems.at[3 * STEPS])
    copies = []
    for step in range(STEPS):
        early = STEP
        late_at = 992 + step * STEP
        late = min(STEP + 16, SAMPLES - late_at)
        copies.append(
            [
                pltpu.make_async_copy(
                    table_hbm.at[step], table_ref.at[step], in_sems.at[3 * step]
                ),
                pltpu.make_async_copy(
                    samples_hbm.at[:, pl.ds(step * STEP, early), :],
                    early_ref.at[step, :, pl.ds(0, early), :],
                    in_sems.at[3 * step + 1],
                ),
                pltpu.make_async_copy(
                    samples_hbm.at[:, pl.ds(late_at, late), :],
                    late_ref.at[step, :, pl.ds(0, late), :],
                    in_sems.at[3 * step + 2],
                ),
            ]
        )
        for copy in copies[-1]:
            copy.start()
    weights_copy.start()

    row = lax.broadcasted_iota(jnp.int32, (SLOT, STEP), 0)
    sign = jnp.where(row % 2 == 0, -1.0, 1.0).astype(BF16)
    tile_row = lax.broadcasted_iota(jnp.int32, (TILE, OFFS), 0)
    upper_half = tile_row < 4
    upper_pair = tile_row % 4 < 2
    missing = HALF - (STEPS - 1) * STEP + 8
    late_ref[STEPS - 1, :, missing:, :] = jnp.zeros(
        (LOCAL_WINDOWS, STEP + 16 - missing, OFFS), BF16
    )
    powers = None
    for step in range(STEPS):
        for copy in copies[step]:
            copy.wait()
        table = table_ref[step]
        turned = (table.reshape(ROWS // SLOT, SLOT, STEP) * sign[None]).reshape(ROWS, STEP)
        pair = jnp.concatenate([table, turned], axis=1)
        samples = jnp.concatenate(
            [
                jnp.concatenate(
                    [early_ref[step, w], late_ref[step, w, 8 : 8 + STEP, :]], axis=0
                )
                for w in range(LOCAL_WINDOWS)
            ],
            axis=1,
        )
        raw = jnp.dot(pair, samples, preferred_element_type=F32)
        if step > 0:
            raw = raw + raw_ref[...]
        raw_ref[...] = raw
        if step == STEPS - 1:
            powers = jnp.sum((raw * raw).reshape(ROWS // 8, 8, LOCAL_WINDOWS * OFFS), axis=0)

    weights_copy.wait()
    factors = []
    for w in range(LOCAL_WINDOWS):
        power = jnp.sum(powers[:, w * OFFS : (w + 1) * OFFS], axis=0, keepdims=True) / FREQS
        factors.append(weights_ref[...] / jnp.sqrt(power + EPS))
    done = []
    for part in range(OUT_PARTS):
        first = part * (DESTS // OUT_PARTS)
        for pair in range(first // 2, (first + DESTS // OUT_PARTS) // 2):
            values = [
                raw_ref[pair * SENT : (pair + 1) * SENT, w * OFFS : (w + 1) * OFFS] * factors[w]
                for w in range(LOCAL_WINDOWS)
            ]
            mixed = [value[3 * TILE : 4 * TILE] for value in values]
            for odd in range(2):
                one, two = [value[4 * odd * TILE : (4 * odd + 3) * TILE] for value in values]
                ends = [one[2 * TILE :], two[2 * TILE :]]
                pieces = [
                    one[: 2 * TILE],
                    two[: 2 * TILE],
                    jnp.where(upper_half, ends[0], pltpu.roll(ends[1], 4, 0)),
                    jnp.where(upper_half, pltpu.roll(ends[0], 4, 0), ends[1]),
                ]
                if odd == 0:
                    pieces.append(jnp.where(upper_pair, mixed[0], pltpu.roll(mixed[1], 2, 0)))
                else:
                    pieces.append(jnp.where(upper_pair, pltpu.roll(mixed[0], 6, 0), mixed[1]))
                out_ref[2 * pair + odd] = jnp.concatenate(pieces, axis=0).astype(BF16)
        here = pl.ds(first, DESTS // OUT_PARTS)
        done.append(pltpu.make_async_copy(out_ref.at[here], out_hbm.at[here], out_sems.at[part]))
        done[-1].start()
    for copy in done:
        copy.wait()


OUT_PARTS = 4


def whiten(samples, weights, table):
    return pl.pallas_call(
        whiten_kernel,
        in_specs=[pl.BlockSpec(memory_space=pl.ANY)] * 3,
        out_specs=pl.BlockSpec(memory_space=pl.ANY),
        out_shape=jax.ShapeDtypeStruct((DESTS, SENT, OFFS), BF16),
        scratch_shapes=[
            pltpu.VMEM((STEPS, LOCAL_WINDOWS, STEP, OFFS), BF16),
            pltpu.VMEM((STEPS, LOCAL_WINDOWS, STEP + 16, OFFS), BF16),
            pltpu.VMEM((STEPS, ROWS, STEP), BF16),
            pltpu.VMEM((1, OFFS), F32),
            pltpu.VMEM((ROWS, LOCAL_WINDOWS * OFFS), F32),
            pltpu.VMEM((DESTS, SENT, OFFS), BF16),
            pltpu.SemaphoreType.DMA((3 * STEPS + 1,)),
            pltpu.SemaphoreType.DMA((OUT_PARTS,)),
        ],
        compiler_params=pltpu.CompilerParams(vmem_limit_bytes=62 << 20),
        cost_estimate=pl.CostEstimate(
            flops=2 * ROWS * SAMPLES * 512, bytes_accessed=5 << 20, transcendentals=0
        ),
        name="whiten",
    )(samples, table, weights)


GROUP = WIN_DEVICES * TAKEN
WAVES = 2 * OFFS


def side_by_side(slot):
    values = slot.astype(F32)
    tiles = [values[at * TILE : (at + 1) * TILE] for at in range(7)]
    real = jnp.concatenate([tiles[0], tiles[2], tiles[4], tiles[6]], axis=0)
    imag = jnp.concatenate(
        [tiles[1], tiles[3], tiles[5], pltpu.roll(tiles[6], 4, 0)], axis=0
    )
    return jnp.concatenate([real, imag], axis=1).astype(BF16)


def by_bin(values):
    tile_row = lax.broadcasted_iota(jnp.int32, (TILE, values.shape[1]), 0)
    tiles = [values[at * TILE : (at + 1) * TILE] for at in range(4)]
    four = tiles[2] + pltpu.roll(tiles[2], 4, 0)
    two = pltpu.roll(tiles[3] + pltpu.roll(tiles[3], 6, 0), 4, 0)
    rest = jnp.where(tile_row < 4, four, jnp.where(tile_row < 6, two, 0.0))
    return jnp.concatenate([tiles[0] + tiles[1], rest], axis=0)


def own_kernel(recv_ref, table_ref, last_ref, cross_ref, slots_ref, waves_ref):
    for source in range(DESTS):
        slots_ref[source * TAKEN : (source + 1) * TAKEN] = side_by_side(recv_ref[source])
    waves_ref[...] = jnp.dot(slots_ref[...], table_ref[...], preferred_element_type=F32)
    last_ref[...] = waves_ref[(SEG_BLOCKS - 1) * GROUP :, :]
    for half in range(2):
        real_at = half * OFFS
        imag_at = WAVES + half * OFFS

        def body(step, total, real_at=real_at, imag_at=imag_at, half=half):
            row = pl.multiple_of(step * TAKEN, TAKEN)
            total_real, total_imag = total
            own_real = waves_ref[pl.ds(row, TAKEN), real_at : real_at + OFFS]
            own_imag = waves_ref[pl.ds(row, TAKEN), imag_at : imag_at + OFFS]
            for block in range(SEG_BLOCKS):
                if block == SEG_BLOCKS - 1:
                    total_real = total_real + (own_real * own_real + own_imag * own_imag)
                    continue
                at = row + (block + 1) * GROUP
                next_real = waves_ref[pl.ds(at, TAKEN), real_at : real_at + OFFS]
                next_imag = waves_ref[pl.ds(at, TAKEN), imag_at : imag_at + OFFS]
                if half == 0:
                    ext_real, ext_imag = own_real + next_real, own_imag + next_imag
                else:
                    ext_real, ext_imag = own_real - next_real, own_imag - next_imag
                total_real = total_real + (own_real * ext_real + own_imag * ext_imag)
                total_imag = total_imag + (own_imag * ext_real - own_real * ext_imag)
                own_real, own_imag = next_real, next_imag
            return total_real, total_imag

        zero = jnp.zeros((TAKEN, OFFS), F32)
        total = lax.fori_loop(0, WIN_DEVICES, body, (zero, zero))
        cross_ref[:, real_at : real_at + OFFS] = total[0]
        cross_ref[:, imag_at : imag_at + OFFS] = total[1]


def own_products(received, table):
    return pl.pallas_call(
        own_kernel,
        out_shape=(
            jax.ShapeDtypeStruct((GROUP, 2 * WAVES), F32),
            jax.ShapeDtypeStruct((TAKEN, 2 * WAVES), F32),
        ),
        in_specs=[pl.BlockSpec(memory_space=pltpu.VMEM)] * 2,
        out_specs=(pl.BlockSpec(memory_space=pltpu.VMEM),) * 2,
        scratch_shapes=[
            pltpu.VMEM((DESTS * TAKEN, WAVES), BF16),
            pltpu.VMEM((DESTS * TAKEN, 2 * WAVES), F32),
        ],
        compiler_params=pltpu.CompilerParams(vmem_limit_bytes=40 << 20),
        cost_estimate=pl.CostEstimate(
            flops=2 * 1024 * 512 * 1024, bytes_accessed=8 << 20, transcendentals=0
        ),
        name="own_products",
    )(received, table)


def image_kernel(
    halo_ref,
    table_ref,
    last_ref,
    cross_ref,
    lead_ref,
    spread_ref,
    fine_ref,
    coarse_ref,
    out_ref,
):
    totals = [
        cross_ref[:, at * OFFS : (at + 1) * OFFS] for at in range(4)
    ]
    spectra = jnp.concatenate([side_by_side(halo_ref[w]) for w in range(WIN_DEVICES)], axis=0)
    waves = jnp.dot(spectra, table_ref[...], preferred_element_type=F32)
    for half in range(2):
        real_at = half * OFFS
        imag_at = WAVES + half * OFFS
        next_real = waves[:, real_at : real_at + OFFS]
        next_imag = waves[:, imag_at : imag_at + OFFS]
        own_real = last_ref[:, real_at : real_at + OFFS]
        own_imag = last_ref[:, imag_at : imag_at + OFFS]
        more_real = own_real * next_real + own_imag * next_imag
        more_imag = own_imag * next_real - own_real * next_imag
        more_real = jnp.sum(more_real.reshape(WIN_DEVICES, TAKEN, OFFS), axis=0)
        more_imag = jnp.sum(more_imag.reshape(WIN_DEVICES, TAKEN, OFFS), axis=0)
        sign = 1.0 if half == 0 else -1.0
        totals[half] = totals[half] + sign * more_real
        totals[2 + half] = totals[2 + half] + sign * more_imag
    cross = by_bin(jnp.concatenate(totals, axis=1))
    flat_real = jnp.sum(cross[:, :WAVES], axis=1, keepdims=True) / WAVES
    flat_imag = jnp.sum(cross[:, WAVES:], axis=1, keepdims=True) / WAVES
    cross = jnp.concatenate([cross[:, :WAVES] - flat_real, cross[:, WAVES:] - flat_imag], axis=1)
    upper = cross.astype(BF16)
    lower = (cross - upper.astype(F32)).astype(BF16)
    both = jnp.concatenate([upper, lower], axis=0)
    stack = jnp.dot(both, lead_ref[...], preferred_element_type=F32)
    stack = stack[:SLOT] + stack[SLOT:]
    lag = lax.broadcasted_iota(jnp.int32, (SLOT, 2 * OFFS), 1)
    stack = stack + jnp.where(lag == 0, flat_real, jnp.where(lag == OFFS, flat_imag, 0.0))
    real = stack[:, :OFFS]
    imag = stack[:, OFFS:]
    power = jnp.sum(real * real + imag * imag, axis=1, keepdims=True) / OFFS
    factor = 1.0 / jnp.sqrt(power + EPS)
    size = SLOT * DIGIT
    row = lax.broadcasted_iota(jnp.int32, (size, OFFS), 0)
    lane = lax.broadcasted_iota(jnp.int32, (size, OFFS), 1)
    same_digit = row // SLOT == lane // DIGIT
    same_bin = row % SLOT == lane // DIGIT

    def spread(values):
        normed = values * factor
        repeated = jnp.broadcast_to(normed[None], (DIGIT, SLOT, OFFS)).reshape(size, OFFS)
        picked = jnp.where(same_digit, repeated, 0.0).astype(BF16)
        moved = jnp.dot(picked, spread_ref[...], preferred_element_type=F32)
        return jnp.where(same_bin, moved, 0.0).astype(BF16)

    of_both = jnp.dot(
        jnp.concatenate([spread(real), spread(imag)], axis=0),
        fine_ref[...],
        preferred_element_type=F32,
    )
    part_real = of_both[:size, :VEL] + of_both[size:, VEL:]
    part_imag = of_both[size:, :VEL] - of_both[:size, VEL:]
    coarse_cos = coarse_ref[:, :VEL]
    coarse_sin = coarse_ref[:, VEL:]
    along = part_real * coarse_cos + part_imag * coarse_sin
    across = part_imag * coarse_cos - part_real * coarse_sin
    along = jnp.sum(along.reshape(DIGIT, SLOT, VEL), axis=0)
    across = jnp.sum(across.reshape(DIGIT, SLOT, VEL), axis=0)
    image = (along * along + across * across) / OFFS
    here = VEL // SEG_BLOCKS
    for block in range(SEG_BLOCKS):
        pair = image[:, block // 2 * LANES : (block // 2 + 1) * LANES]
        out_ref[block] = pair if block % 2 == 0 else jnp.roll(pair, here, axis=1)


def image_of(halo, table, last, cross, lead, spread, fine, coarse):
    return pl.pallas_call(
        image_kernel,
        out_shape=jax.ShapeDtypeStruct((SEG_BLOCKS, SLOT, LANES), F32),
        in_specs=[pl.BlockSpec(memory_space=pltpu.VMEM)] * 8,
        out_specs=pl.BlockSpec(memory_space=pltpu.VMEM),
        compiler_params=pltpu.CompilerParams(vmem_limit_bytes=40 << 20),
        cost_estimate=pl.CostEstimate(
            flops=2 * 700 * 512 * 1024, bytes_accessed=6 << 20, transcendentals=0
        ),
        name="image",
    )(halo, table, last, cross, lead, spread, fine, coarse)


def gather(parts, table):
    rows = parts.reshape(SEG_BLOCKS * SLOT, LANES)
    gathered = lax.dot_general(
        rows,
        table,
        (((0,), (0,)), ((), ())),
        precision=lax.Precision.HIGHEST,
        preferred_element_type=F32,
    )
    return gathered[: VEL // SEG_BLOCKS]


def local(samples_data, coupling):
    whitened = whiten(samples_data, coupling[None, :], jnp.asarray(time_table()))
    received = lax.all_to_all(whitened, ("blk", "win"), 0, 0, tiled=True)
    segments = lax.axis_size("seg")
    first_block = received[:WIN_DEVICES]
    halo = lax.ppermute(first_block, "seg", [(s, s - 1) for s in range(1, segments)])
    table = jnp.asarray(forward_table())
    last, cross = own_products(received, table)
    fine, coarse = basis_tables(lax.axis_index("blk"), lax.axis_index("win"))
    parts = image_of(
        halo,
        table,
        last,
        cross,
        jnp.asarray(inverse_table()),
        jnp.asarray(spread_table()),
        fine,
        coarse,
    )
    parts = lax.all_to_all(parts, "blk", 0, 0, tiled=True)
    return gather(parts, jnp.asarray(gather_table()))


def solution(mesh):
    segments = mesh.shape["fibre"] // SEG_BLOCKS
    inner = Mesh(
        mesh.devices.reshape(segments, SEG_BLOCKS, mesh.shape["win"]), ("seg", "blk", "win")
    )
    placed = (P("win", None, ("seg", "blk")), P(("seg", "blk")))
    return jax.shard_map(
        local, mesh=inner, in_specs=placed, out_specs=P(("seg", "blk"), "win"), check_vma=False
    )
```

```python
import math

import jax
import jax.numpy as jnp
import ml_dtypes
import numpy as np
from jax import lax
from jax.experimental import pallas as pl
from jax.experimental.pallas import tpu as pltpu
from jax.sharding import Mesh, PartitionSpec as P

SAMPLES = 2000
FREQS = 400
OFFS = 256
VEL = 512
SEG_BLOCKS = 8
EPS = 1e-06

WIN_DEVICES = 4
DESTS = SEG_BLOCKS * WIN_DEVICES
CHUNK = FREQS // WIN_DEVICES
FIRST_BIN = [0, 13, 25, 38, 50, 63, 75, 88, CHUNK]
SLOT = 16
TILE = 8
SENT = 13 * TILE
TAKEN = 4 * TILE
LOCAL_WINDOWS = 2
DIGIT = 16
ROWS = SEG_BLOCKS * 13 * TILE
LANES = 128
STEP = 256
STEPS = 4
HALF = SAMPLES // 2
BF16 = jnp.bfloat16
F32 = jnp.float32


def bins_of(block, window_device):
    rows = np.arange(SLOT)
    within = FIRST_BIN[block] + rows
    return np.where(within < FIRST_BIN[block + 1], window_device * CHUNK + within, -1)


def table_rows():
    bins, parts = [], []
    for block in range(SEG_BLOCKS):
        dests = [bins_of(block, window_device) for window_device in range(WIN_DEVICES)]
        rows = []
        for dest in dests:
            for first, last in ((0, 8), (8, 12)):
                for part in (0, 1):
                    rows += [(dest[r], part) for r in range(first, last)]
        rows += [(dest[12], part) for part in (0, 1) for dest in dests]
        for at, part in rows:
            bins.append(at)
            parts.append(part)
    return np.array(bins), np.array(parts)


def time_table():
    bins, parts = table_rows()
    times = np.arange(STEP * STEPS, dtype=np.int64)
    turns = ((bins[:, None] + 1) * times[None, :]) % SAMPLES
    angle = np.float32(2.0 * math.pi / SAMPLES) * turns.astype(np.float32)
    valid = (bins >= 0)[:, None] & (times < SAMPLES // 2)[None, :]
    waves = np.where(parts[:, None] == 0, np.cos(angle), -np.sin(angle))
    table = np.where(valid, waves, 0.0).reshape(ROWS, STEPS, STEP)
    return table.transpose(1, 0, 2).astype(np.float32).astype(ml_dtypes.bfloat16)


def wave_order():
    return np.concatenate([np.arange(0, 2 * OFFS, 2), np.arange(1, 2 * OFFS, 2)])


def forward_table():
    rows = np.arange(OFFS)
    angle = 2.0 * np.pi / (2 * OFFS) * ((rows[:, None] * wave_order()[None, :]) % (2 * OFFS))
    cosines, sines = np.cos(angle), np.sin(angle)
    upper = np.concatenate([cosines, -sines], axis=1)
    lower = np.concatenate([sines, cosines], axis=1)
    return np.concatenate([upper, lower], axis=0).astype(np.float32).astype(ml_dtypes.bfloat16)


def inverse_table():
    lags = np.arange(OFFS)
    angle = 2.0 * np.pi / (2 * OFFS) * ((wave_order()[:, None] * lags[None, :]) % (2 * OFFS))
    cosines, sines = np.cos(angle), np.sin(angle)
    upper = np.concatenate([cosines, -sines], axis=1)
    lower = np.concatenate([sines, cosines], axis=1)
    full = (np.concatenate([upper, lower], axis=0) / (2 * OFFS)).astype(np.float32)
    return full.astype(ml_dtypes.bfloat16)


def spread_table():
    index = np.arange(OFFS)
    same = (index[:, None] % DIGIT) == (index[None, :] % DIGIT)
    return same.astype(ml_dtypes.bfloat16)


def gather_table():
    table = np.zeros((SEG_BLOCKS * SLOT, CHUNK), np.float32)
    for block in range(SEG_BLOCKS):
        for row in range(FIRST_BIN[block + 1] - FIRST_BIN[block]):
            table[block * SLOT + row, FIRST_BIN[block] + row] = 1.0
    return table


def turn_waves(turns):
    rest = turns - jnp.round(turns)
    half = rest * math.pi
    square = half * half
    sine = half * (
        1.0
        + square
        * (
            -1.0 / 6
            + square
            * (1.0 / 120 + square * (-1.0 / 5040 + square * (1.0 / 362880 - square / 39916800)))
        )
    )
    cosine = 1.0 + square * (
        -0.5
        + square
        * (
            1.0 / 24
            + square
            * (
                -1.0 / 720
                + square * (1.0 / 40320 + square * (-1.0 / 3628800 + square / 479001600))
            )
        )
    )
    return 1.0 - 2.0 * sine * sine, 2.0 * sine * cosine


def basis_tables(block, window_device):
    speeds = jnp.arange(VEL, dtype=jnp.int32)
    speed = 150.0 + 1350.0 * speeds.astype(F32) / (VEL - 1)
    slowness = (200.0 * 8.0 / SAMPLES / speed)[None, :]
    first = window_device * CHUNK + (25 * block + 1) // 2 + 1
    index = jnp.arange(SLOT * DIGIT, dtype=jnp.int32)
    fine = ((first + index // DIGIT) * (index % DIGIT)).astype(F32)[:, None]
    coarse = ((first + index % SLOT) * (index // SLOT * DIGIT)).astype(F32)[:, None]
    fine_cos, fine_sin = turn_waves(fine * slowness)
    coarse_cos, coarse_sin = turn_waves(coarse * slowness)
    fine_table = jnp.concatenate([fine_cos, fine_sin], axis=1).astype(BF16)
    coarse_table = jnp.concatenate([coarse_cos, coarse_sin], axis=1)
    return fine_table, coarse_table


def whiten_kernel(
    samples_hbm,
    table_hbm,
    weights_hbm,
    out_hbm,
    early_ref,
    late_ref,
    table_ref,
    weights_ref,
    raw_ref,
    out_ref,
    in_sems,
    out_sems,
):
    weights_copy = pltpu.make_async_copy(weights_hbm, weights_ref, in_sems.at[3 * STEPS])
    copies = []
    for step in range(STEPS):
        early = STEP
        late_at = 992 + step * STEP
        late = min(STEP + 16, SAMPLES - late_at)
        copies.append(
            [
                pltpu.make_async_copy(
                    table_hbm.at[step], table_ref.at[step], in_sems.at[3 * step]
                ),
                pltpu.make_async_copy(
                    samples_hbm.at[:, pl.ds(step * STEP, early), :],
                    early_ref.at[step, :, pl.ds(0, early), :],
                    in_sems.at[3 * step + 1],
                ),
                pltpu.make_async_copy(
                    samples_hbm.at[:, pl.ds(late_at, late), :],
                    late_ref.at[step, :, pl.ds(0, late), :],
                    in_sems.at[3 * step + 2],
                ),
            ]
        )
        for copy in copies[-1]:
            copy.start()
    weights_copy.start()

    row = lax.broadcasted_iota(jnp.int32, (ROWS // SEG_BLOCKS, STEP), 0)
    odd = jnp.where((row % 2 == 0) | (row >= 12 * TILE), -1.0, 1.0)
    sign = jnp.concatenate(
        [odd if FIRST_BIN[block] % 2 == 0 else -odd for block in range(SEG_BLOCKS)], axis=0
    ).astype(BF16)
    tile_row = lax.broadcasted_iota(jnp.int32, (TILE, OFFS), 0)
    upper_half = tile_row < 4
    missing = HALF - (STEPS - 1) * STEP + 8
    late_ref[STEPS - 1, :, missing:, :] = jnp.zeros(
        (LOCAL_WINDOWS, STEP + 16 - missing, OFFS), BF16
    )
    powers = None
    for step in range(STEPS):
        for copy in copies[step]:
            copy.wait()
        table = table_ref[step]
        turned = table * sign
        pair = jnp.concatenate([table, turned], axis=1)
        samples = jnp.concatenate(
            [
                jnp.concatenate(
                    [early_ref[step, w], late_ref[step, w, 8 : 8 + STEP, :]], axis=0
                )
                for w in range(LOCAL_WINDOWS)
            ],
            axis=1,
        )
        raw = jnp.dot(pair, samples, preferred_element_type=F32)
        if step > 0:
            raw = raw + raw_ref[...]
        raw_ref[...] = raw
        if step == STEPS - 1:
            powers = jnp.sum((raw * raw).reshape(ROWS // 8, 8, LOCAL_WINDOWS * OFFS), axis=0)

    weights_copy.wait()
    factors = []
    for w in range(LOCAL_WINDOWS):
        power = jnp.sum(powers[:, w * OFFS : (w + 1) * OFFS], axis=0, keepdims=True) / FREQS
        factors.append(weights_ref[...] / jnp.sqrt(power + EPS))
    done = []
    for part in range(OUT_PARTS):
        first = part * (DESTS // OUT_PARTS)
        for block in range(first // WIN_DEVICES, (first + DESTS // OUT_PARTS) // WIN_DEVICES):
            rows = slice(block * 13 * TILE, (block + 1) * 13 * TILE)
            values = [
                raw_ref[rows, w * OFFS : (w + 1) * OFFS] * factors[w]
                for w in range(LOCAL_WINDOWS)
            ]
            final = [value[12 * TILE :] for value in values]
            for dest in range(WIN_DEVICES):
                one, two = [
                    value[3 * dest * TILE : 3 * (dest + 1) * TILE] for value in values
                ]
                ends = [one[2 * TILE :], two[2 * TILE :]]
                six = jnp.concatenate(
                    [
                        one[: 2 * TILE],
                        two[: 2 * TILE],
                        jnp.where(upper_half, ends[0], pltpu.roll(ends[1], 4, 0)),
                        jnp.where(upper_half, pltpu.roll(ends[0], 4, 0), ends[1]),
                    ],
                    axis=0,
                )
                moved = [
                    pltpu.roll(final[at % 2], (at - at // 2 * 4 - dest) % TILE, 0)
                    for at in range(4)
                ]
                mixed = moved[3]
                for at in range(3):
                    mixed = jnp.where(tile_row == at, moved[at], mixed)
                mixed = jnp.where(
                    upper_half[:, :LANES],
                    mixed[:, :LANES],
                    pltpu.roll(mixed[:, LANES:], 4, 0),
                )
                out_ref[block * WIN_DEVICES + dest] = jnp.concatenate(
                    [six[:, :LANES], six[:, LANES:], mixed], axis=0
                ).astype(BF16)
        here = pl.ds(first, DESTS // OUT_PARTS)
        done.append(pltpu.make_async_copy(out_ref.at[here], out_hbm.at[here], out_sems.at[part]))
        done[-1].start()
    for copy in done:
        copy.wait()


OUT_PARTS = 4


def whiten(samples, weights, table):
    return pl.pallas_call(
        whiten_kernel,
        in_specs=[pl.BlockSpec(memory_space=pl.ANY)] * 3,
        out_specs=pl.BlockSpec(memory_space=pl.ANY),
        out_shape=jax.ShapeDtypeStruct((DESTS, SENT, LANES), BF16),
        scratch_shapes=[
            pltpu.VMEM((STEPS, LOCAL_WINDOWS, STEP, OFFS), BF16),
            pltpu.VMEM((STEPS, LOCAL_WINDOWS, STEP + 16, OFFS), BF16),
            pltpu.VMEM((STEPS, ROWS, STEP), BF16),
            pltpu.VMEM((1, OFFS), F32),
            pltpu.VMEM((ROWS, LOCAL_WINDOWS * OFFS), F32),
            pltpu.VMEM((DESTS, SENT, LANES), BF16),
            pltpu.SemaphoreType.DMA((3 * STEPS + 1,)),
            pltpu.SemaphoreType.DMA((OUT_PARTS,)),
        ],
        compiler_params=pltpu.CompilerParams(vmem_limit_bytes=62 << 20),
        cost_estimate=pl.CostEstimate(
            flops=2 * ROWS * SAMPLES * 512, bytes_accessed=5 << 20, transcendentals=0
        ),
        name="whiten",
    )(samples, table, weights)


GROUP = WIN_DEVICES * TAKEN
WAVES = 2 * OFFS


def side_by_side(slot):
    values = slot.astype(F32)
    six = jnp.concatenate([values[: 6 * TILE], values[6 * TILE : 12 * TILE]], axis=1)
    tiles = [six[at * TILE : (at + 1) * TILE] for at in range(6)]
    mixed = values[12 * TILE :]
    real = jnp.concatenate([mixed, pltpu.roll(mixed, 4, 0)], axis=1)
    imag = jnp.concatenate([pltpu.roll(mixed, 6, 0), pltpu.roll(mixed, 2, 0)], axis=1)
    real = jnp.concatenate([tiles[0], tiles[2], tiles[4], real], axis=0)
    imag = jnp.concatenate([tiles[1], tiles[3], tiles[5], imag], axis=0)
    return jnp.concatenate([real, imag], axis=1).astype(BF16)


def by_bin(values):
    tile_row = lax.broadcasted_iota(jnp.int32, (TILE, values.shape[1]), 0)
    tiles = [values[at * TILE : (at + 1) * TILE] for at in range(4)]
    four = tiles[2] + pltpu.roll(tiles[2], 4, 0)
    one = pltpu.roll(tiles[3] + pltpu.roll(tiles[3], 7, 0), 4, 0)
    rest = jnp.where(tile_row < 4, four, jnp.where(tile_row == 4, one, 0.0))
    return jnp.concatenate([tiles[0] + tiles[1], rest], axis=0)


def own_kernel(recv_ref, table_ref, last_ref, cross_ref, slots_ref, waves_ref):
    for source in range(DESTS):
        slots_ref[source * TAKEN : (source + 1) * TAKEN] = side_by_side(recv_ref[source])
    waves_ref[...] = jnp.dot(slots_ref[...], table_ref[...], preferred_element_type=F32)
    last_ref[...] = waves_ref[(SEG_BLOCKS - 1) * GROUP :, :]
    for half in range(2):
        real_at = half * OFFS
        imag_at = WAVES + half * OFFS

        def body(step, total, real_at=real_at, imag_at=imag_at, half=half):
            row = pl.multiple_of(step * TAKEN, TAKEN)
            total_real, total_imag = total
            own_real = waves_ref[pl.ds(row, TAKEN), real_at : real_at + OFFS]
            own_imag = waves_ref[pl.ds(row, TAKEN), imag_at : imag_at + OFFS]
            for block in range(SEG_BLOCKS):
                if block == SEG_BLOCKS - 1:
                    total_real = total_real + (own_real * own_real + own_imag * own_imag)
                    continue
                at = row + (block + 1) * GROUP
                next_real = waves_ref[pl.ds(at, TAKEN), real_at : real_at + OFFS]
                next_imag = waves_ref[pl.ds(at, TAKEN), imag_at : imag_at + OFFS]
                if half == 0:
                    ext_real, ext_imag = own_real + next_real, own_imag + next_imag
                else:
                    ext_real, ext_imag = own_real - next_real, own_imag - next_imag
                total_real = total_real + (own_real * ext_real + own_imag * ext_imag)
                total_imag = total_imag + (own_imag * ext_real - own_real * ext_imag)
                own_real, own_imag = next_real, next_imag
            return total_real, total_imag

        zero = jnp.zeros((TAKEN, OFFS), F32)
        total = lax.fori_loop(0, WIN_DEVICES, body, (zero, zero))
        cross_ref[:, real_at : real_at + OFFS] = total[0]
        cross_ref[:, imag_at : imag_at + OFFS] = total[1]


def own_products(received, table):
    return pl.pallas_call(
        own_kernel,
        out_shape=(
            jax.ShapeDtypeStruct((GROUP, 2 * WAVES), F32),
            jax.ShapeDtypeStruct((TAKEN, 2 * WAVES), F32),
        ),
        in_specs=[pl.BlockSpec(memory_space=pltpu.VMEM)] * 2,
        out_specs=(pl.BlockSpec(memory_space=pltpu.VMEM),) * 2,
        scratch_shapes=[
            pltpu.VMEM((DESTS * TAKEN, WAVES), BF16),
            pltpu.VMEM((DESTS * TAKEN, 2 * WAVES), F32),
        ],
        compiler_params=pltpu.CompilerParams(vmem_limit_bytes=40 << 20),
        cost_estimate=pl.CostEstimate(
            flops=2 * 1024 * 512 * 1024, bytes_accessed=8 << 20, transcendentals=0
        ),
        name="own_products",
    )(received, table)


def image_kernel(
    halo_ref,
    table_ref,
    last_ref,
    cross_ref,
    lead_ref,
    spread_ref,
    fine_ref,
    coarse_ref,
    out_ref,
):
    totals = [
        cross_ref[:, at * OFFS : (at + 1) * OFFS] for at in range(4)
    ]
    spectra = jnp.concatenate([side_by_side(halo_ref[w]) for w in range(WIN_DEVICES)], axis=0)
    waves = jnp.dot(spectra, table_ref[...], preferred_element_type=F32)
    for half in range(2):
        real_at = half * OFFS
        imag_at = WAVES + half * OFFS
        next_real = waves[:, real_at : real_at + OFFS]
        next_imag = waves[:, imag_at : imag_at + OFFS]
        own_real = last_ref[:, real_at : real_at + OFFS]
        own_imag = last_ref[:, imag_at : imag_at + OFFS]
        more_real = own_real * next_real + own_imag * next_imag
        more_imag = own_imag * next_real - own_real * next_imag
        more_real = jnp.sum(more_real.reshape(WIN_DEVICES, TAKEN, OFFS), axis=0)
        more_imag = jnp.sum(more_imag.reshape(WIN_DEVICES, TAKEN, OFFS), axis=0)
        sign = 1.0 if half == 0 else -1.0
        totals[half] = totals[half] + sign * more_real
        totals[2 + half] = totals[2 + half] + sign * more_imag
    cross = by_bin(jnp.concatenate(totals, axis=1))
    flat_real = jnp.sum(cross[:, :WAVES], axis=1, keepdims=True) / WAVES
    flat_imag = jnp.sum(cross[:, WAVES:], axis=1, keepdims=True) / WAVES
    cross = jnp.concatenate([cross[:, :WAVES] - flat_real, cross[:, WAVES:] - flat_imag], axis=1)
    upper = cross.astype(BF16)
    lower = (cross - upper.astype(F32)).astype(BF16)
    both = jnp.concatenate([upper, lower], axis=0)
    stack = jnp.dot(both, lead_ref[...], preferred_element_type=F32)
    stack = stack[:SLOT] + stack[SLOT:]
    lag = lax.broadcasted_iota(jnp.int32, (SLOT, 2 * OFFS), 1)
    stack = stack + jnp.where(lag == 0, flat_real, jnp.where(lag == OFFS, flat_imag, 0.0))
    real = stack[:, :OFFS]
    imag = stack[:, OFFS:]
    power = jnp.sum(real * real + imag * imag, axis=1, keepdims=True) / OFFS
    factor = 1.0 / jnp.sqrt(power + EPS)
    size = SLOT * DIGIT
    row = lax.broadcasted_iota(jnp.int32, (size, OFFS), 0)
    lane = lax.broadcasted_iota(jnp.int32, (size, OFFS), 1)
    same_digit = row // SLOT == lane // DIGIT
    same_bin = row % SLOT == lane // DIGIT

    def spread(values):
        normed = values * factor
        repeated = jnp.broadcast_to(normed[None], (DIGIT, SLOT, OFFS)).reshape(size, OFFS)
        picked = jnp.where(same_digit, repeated, 0.0).astype(BF16)
        moved = jnp.dot(picked, spread_ref[...], preferred_element_type=F32)
        return jnp.where(same_bin, moved, 0.0).astype(BF16)

    of_both = jnp.dot(
        jnp.concatenate([spread(real), spread(imag)], axis=0),
        fine_ref[...],
        preferred_element_type=F32,
    )
    part_real = of_both[:size, :VEL] + of_both[size:, VEL:]
    part_imag = of_both[size:, :VEL] - of_both[:size, VEL:]
    coarse_cos = coarse_ref[:, :VEL]
    coarse_sin = coarse_ref[:, VEL:]
    along = part_real * coarse_cos + part_imag * coarse_sin
    across = part_imag * coarse_cos - part_real * coarse_sin
    along = jnp.sum(along.reshape(DIGIT, SLOT, VEL), axis=0)
    across = jnp.sum(across.reshape(DIGIT, SLOT, VEL), axis=0)
    image = (along * along + across * across) / OFFS
    here = VEL // SEG_BLOCKS
    for block in range(SEG_BLOCKS):
        pair = image[:, block // 2 * LANES : (block // 2 + 1) * LANES]
        out_ref[block] = pair if block % 2 == 0 else jnp.roll(pair, here, axis=1)


def image_of(halo, table, last, cross, lead, spread, fine, coarse):
    return pl.pallas_call(
        image_kernel,
        out_shape=jax.ShapeDtypeStruct((SEG_BLOCKS, SLOT, LANES), F32),
        in_specs=[pl.BlockSpec(memory_space=pltpu.VMEM)] * 8,
        out_specs=pl.BlockSpec(memory_space=pltpu.VMEM),
        compiler_params=pltpu.CompilerParams(vmem_limit_bytes=40 << 20),
        cost_estimate=pl.CostEstimate(
            flops=2 * 700 * 512 * 1024, bytes_accessed=6 << 20, transcendentals=0
        ),
        name="image",
    )(halo, table, last, cross, lead, spread, fine, coarse)


def gather(parts, table):
    rows = parts.reshape(SEG_BLOCKS * SLOT, LANES)
    gathered = lax.dot_general(
        rows,
        table,
        (((0,), (0,)), ((), ())),
        precision=lax.Precision.HIGHEST,
        preferred_element_type=F32,
    )
    return gathered[: VEL // SEG_BLOCKS]


def local(samples_data, coupling):
    whitened = whiten(samples_data, coupling[None, :], jnp.asarray(time_table()))
    received = lax.all_to_all(whitened, ("blk", "win"), 0, 0, tiled=True)
    segments = lax.axis_size("seg")
    first_block = received[:WIN_DEVICES]
    halo = lax.ppermute(first_block, "seg", [(s, s - 1) for s in range(1, segments)])
    table = jnp.asarray(forward_table())
    last, cross = own_products(received, table)
    fine, coarse = basis_tables(lax.axis_index("blk"), lax.axis_index("win"))
    parts = image_of(
        halo,
        table,
        last,
        cross,
        jnp.asarray(inverse_table()),
        jnp.asarray(spread_table()),
        fine,
        coarse,
    )
    parts = lax.all_to_all(parts, "blk", 0, 0, tiled=True)
    return gather(parts, jnp.asarray(gather_table()))


def solution(mesh):
    segments = mesh.shape["fibre"] // SEG_BLOCKS
    inner = Mesh(
        mesh.devices.reshape(segments, SEG_BLOCKS, mesh.shape["win"]), ("seg", "blk", "win")
    )
    placed = (P("win", None, ("seg", "blk")), P(("seg", "blk")))
    return jax.shard_map(
        local, mesh=inner, in_specs=placed, out_specs=P(("seg", "blk"), "win"), check_vma=False
    )
```

```python
import math

import jax
import jax.numpy as jnp
import ml_dtypes
import numpy as np
from jax import lax
from jax.experimental import pallas as pl
from jax.experimental.pallas import tpu as pltpu
from jax.sharding import Mesh, PartitionSpec as P

SAMPLES = 2000
FREQS = 400
OFFS = 256
VEL = 512
SEG_BLOCKS = 8
EPS = 1e-06

WIN_DEVICES = 4
DESTS = SEG_BLOCKS * WIN_DEVICES
CHUNK = FREQS // WIN_DEVICES
FIRST_BIN = [0, 13, 25, 38, 50, 63, 75, 88, CHUNK]
SLOT = 16
TILE = 8
SENT = 13 * TILE
TAKEN = 4 * TILE
LOCAL_WINDOWS = 2
DIGIT = 16
ROWS = SEG_BLOCKS * 13 * TILE
LANES = 128
STEP = 256
STEPS = 4
HALF = SAMPLES // 2
BF16 = jnp.bfloat16
F32 = jnp.float32


def bins_of(block, window_device):
    rows = np.arange(SLOT)
    within = FIRST_BIN[block] + rows
    return np.where(within < FIRST_BIN[block + 1], window_device * CHUNK + within, -1)


def table_rows():
    bins, parts = [], []
    for block in range(SEG_BLOCKS):
        dests = [bins_of(block, window_device) for window_device in range(WIN_DEVICES)]
        rows = []
        for dest in dests:
            for first, last in ((0, 8), (8, 12)):
                for part in (0, 1):
                    rows += [(dest[r], part) for r in range(first, last)]
        rows += [(dest[12], part) for part in (0, 1) for dest in dests]
        for at, part in rows:
            bins.append(at)
            parts.append(part)
    return np.array(bins), np.array(parts)


def time_table():
    bins, parts = table_rows()
    times = np.arange(STEP * STEPS, dtype=np.int64)
    turns = ((bins[:, None] + 1) * times[None, :]) % SAMPLES
    angle = np.float32(2.0 * math.pi / SAMPLES) * turns.astype(np.float32)
    valid = (bins >= 0)[:, None] & (times < SAMPLES // 2)[None, :]
    waves = np.where(parts[:, None] == 0, np.cos(angle), -np.sin(angle))
    table = np.where(valid, waves, 0.0).reshape(ROWS, STEPS, STEP)
    return table.transpose(1, 0, 2).astype(np.float32).astype(ml_dtypes.bfloat16)


def wave_order():
    return np.concatenate([np.arange(0, 2 * OFFS, 2), np.arange(1, 2 * OFFS, 2)])


def forward_table(sines_first=False):
    rows = np.arange(OFFS)
    angle = 2.0 * np.pi / (2 * OFFS) * ((rows[:, None] * wave_order()[None, :]) % (2 * OFFS))
    halves = [np.cos(angle), np.sin(angle)]
    table = np.concatenate(halves[::-1] if sines_first else halves, axis=1)
    return table.astype(np.float32).astype(ml_dtypes.bfloat16)


def inverse_table():
    lags = np.arange(OFFS)
    angle = 2.0 * np.pi / (2 * OFFS) * ((wave_order()[:, None] * lags[None, :]) % (2 * OFFS))
    cosines, sines = np.cos(angle), np.sin(angle)
    upper = np.concatenate([cosines, -sines], axis=1)
    lower = np.concatenate([sines, cosines], axis=1)
    full = (np.concatenate([upper, lower], axis=0) / (2 * OFFS)).astype(np.float32)
    return full.astype(ml_dtypes.bfloat16)


def spread_table():
    index = np.arange(OFFS)
    same = (index[:, None] % DIGIT) == (index[None, :] // SLOT)
    return same.astype(ml_dtypes.bfloat16)


def gather_table():
    table = np.zeros((SEG_BLOCKS * SLOT, CHUNK), np.float32)
    for block in range(SEG_BLOCKS):
        for row in range(FIRST_BIN[block + 1] - FIRST_BIN[block]):
            table[block * SLOT + row, FIRST_BIN[block] + row] = 1.0
    return table


def turn_waves(turns):
    rest = turns - jnp.floor(turns + 0.5)
    half = rest * math.pi
    square = half * half
    sine = half * (
        1.0
        + square
        * (
            -1.0 / 6
            + square
            * (1.0 / 120 + square * (-1.0 / 5040 + square * (1.0 / 362880 - square / 39916800)))
        )
    )
    cosine = 1.0 + square * (
        -0.5
        + square
        * (
            1.0 / 24
            + square
            * (
                -1.0 / 720
                + square * (1.0 / 40320 + square * (-1.0 / 3628800 + square / 479001600))
            )
        )
    )
    return 1.0 - 2.0 * sine * sine, 2.0 * sine * cosine


def turns_of(block, window_device):
    speeds = jnp.arange(VEL, dtype=jnp.int32)
    speed = 150.0 + 1350.0 * speeds.astype(F32) / (VEL - 1)
    slowness = (200.0 * 8.0 / SAMPLES / speed)[None, :]
    first = window_device * CHUNK + (25 * block + 1) // 2 + 1
    return (first + jnp.arange(SLOT, dtype=jnp.int32)).astype(F32)[:, None] * slowness


def powers_of(cosine, sine):
    now = (jnp.ones_like(cosine), jnp.zeros_like(sine))
    waves = [now]
    for _ in range(DIGIT - 1):
        now = (now[0] * cosine - now[1] * sine, now[1] * cosine + now[0] * sine)
        waves.append(now)
    return waves


def whiten_kernel(
    samples_hbm,
    table_hbm,
    weights_hbm,
    out_ref,
    early_ref,
    late_ref,
    table_ref,
    weights_ref,
    raw_ref,
    in_sems,
):
    weights_copy = pltpu.make_async_copy(weights_hbm, weights_ref, in_sems.at[3 * STEPS])
    copies = []
    for step in range(STEPS):
        early = STEP
        late_at = 992 + step * STEP
        late = min(STEP + 16, SAMPLES - late_at)
        copies.append(
            [
                pltpu.make_async_copy(
                    table_hbm.at[step], table_ref.at[step], in_sems.at[3 * step]
                ),
                pltpu.make_async_copy(
                    samples_hbm.at[:, pl.ds(step * STEP, early), :],
                    early_ref.at[step, :, pl.ds(0, early), :],
                    in_sems.at[3 * step + 1],
                ),
                pltpu.make_async_copy(
                    samples_hbm.at[:, pl.ds(late_at, late), :],
                    late_ref.at[step, :, pl.ds(0, late), :],
                    in_sems.at[3 * step + 2],
                ),
            ]
        )
        for copy in copies[-1]:
            copy.start()
    weights_copy.start()

    row = lax.broadcasted_iota(jnp.int32, (ROWS // SEG_BLOCKS, STEP), 0)
    odd = jnp.where((row % 2 == 0) | (row >= 12 * TILE), -1.0, 1.0)
    sign = jnp.concatenate(
        [odd if FIRST_BIN[block] % 2 == 0 else -odd for block in range(SEG_BLOCKS)], axis=0
    ).astype(BF16)
    tile_row = lax.broadcasted_iota(jnp.int32, (TILE, OFFS), 0)
    upper_half = tile_row < 4
    missing = HALF - (STEPS - 1) * STEP + 8
    late_ref[STEPS - 1, :, missing:, :] = jnp.zeros(
        (LOCAL_WINDOWS, STEP + 16 - missing, OFFS), BF16
    )
    powers = None
    for step in range(STEPS):
        for copy in copies[step]:
            copy.wait()
        table = table_ref[step]
        turned = table * sign
        pair = jnp.concatenate([table, turned], axis=1)
        samples = jnp.concatenate(
            [
                jnp.concatenate(
                    [early_ref[step, w], late_ref[step, w, 8 : 8 + STEP, :]], axis=0
                )
                for w in range(LOCAL_WINDOWS)
            ],
            axis=1,
        )
        raw = jnp.dot(pair, samples, preferred_element_type=F32)
        if step > 0:
            raw = raw + raw_ref[...]
        raw_ref[...] = raw
        if step == STEPS - 1:
            powers = jnp.sum((raw * raw).reshape(ROWS // 8, 8, LOCAL_WINDOWS * OFFS), axis=0)

    weights_copy.wait()
    factors = []
    for w in range(LOCAL_WINDOWS):
        power = jnp.sum(powers[:, w * OFFS : (w + 1) * OFFS], axis=0, keepdims=True) / FREQS
        factors.append(weights_ref[...] / jnp.sqrt(power + EPS))
    for block in range(SEG_BLOCKS):
        rows = slice(block * 13 * TILE, (block + 1) * 13 * TILE)
        values = [
            raw_ref[rows, w * OFFS : (w + 1) * OFFS] * factors[w]
            for w in range(LOCAL_WINDOWS)
        ]
        final = [value[12 * TILE :] for value in values]
        for dest in range(WIN_DEVICES):
            one, two = [
                value[3 * dest * TILE : 3 * (dest + 1) * TILE] for value in values
            ]
            ends = [one[2 * TILE :], two[2 * TILE :]]
            six = jnp.concatenate(
                [
                    one[: 2 * TILE],
                    two[: 2 * TILE],
                    jnp.where(upper_half, ends[0], pltpu.roll(ends[1], 4, 0)),
                    jnp.where(upper_half, pltpu.roll(ends[0], 4, 0), ends[1]),
                ],
                axis=0,
            )
            moved = [
                pltpu.roll(final[at % 2], (at - at // 2 * 4 - dest) % TILE, 0)
                for at in range(4)
            ]
            mixed = moved[3]
            for at in range(3):
                mixed = jnp.where(tile_row == at, moved[at], mixed)
            mixed = jnp.where(
                upper_half[:, :LANES],
                mixed[:, :LANES],
                pltpu.roll(mixed[:, LANES:], 4, 0),
            )
            out_ref[block * WIN_DEVICES + dest] = jnp.concatenate(
                [six[:, :LANES], six[:, LANES:], mixed], axis=0
            ).astype(BF16)


def whiten(samples, weights, table):
    return pl.pallas_call(
        whiten_kernel,
        in_specs=[pl.BlockSpec(memory_space=pl.ANY)] * 3,
        out_specs=pl.BlockSpec(memory_space=pltpu.VMEM),
        out_shape=jax.ShapeDtypeStruct((DESTS, SENT, LANES), BF16),
        scratch_shapes=[
            pltpu.VMEM((STEPS, LOCAL_WINDOWS, STEP, OFFS), BF16),
            pltpu.VMEM((STEPS, LOCAL_WINDOWS, STEP + 16, OFFS), BF16),
            pltpu.VMEM((STEPS, ROWS, STEP), BF16),
            pltpu.VMEM((1, OFFS), F32),
            pltpu.VMEM((ROWS, LOCAL_WINDOWS * OFFS), F32),
            pltpu.SemaphoreType.DMA((3 * STEPS + 1,)),
        ],
        compiler_params=pltpu.CompilerParams(vmem_limit_bytes=62 << 20),
        cost_estimate=pl.CostEstimate(
            flops=2 * ROWS * SAMPLES * 512, bytes_accessed=5 << 20, transcendentals=0
        ),
        name="whiten",
    )(samples, table, weights)


GROUP = WIN_DEVICES * TAKEN
WAVES = 2 * OFFS


def parts_of(slot):
    values = slot.astype(F32)
    six = jnp.concatenate([values[: 6 * TILE], values[6 * TILE : 12 * TILE]], axis=1)
    tiles = [six[at * TILE : (at + 1) * TILE] for at in range(6)]
    mixed = values[12 * TILE :]
    real = jnp.concatenate([mixed, pltpu.roll(mixed, 4, 0)], axis=1)
    imag = jnp.concatenate([pltpu.roll(mixed, 6, 0), pltpu.roll(mixed, 2, 0)], axis=1)
    real = jnp.concatenate([tiles[0], tiles[2], tiles[4], real], axis=0)
    imag = jnp.concatenate([tiles[1], tiles[3], tiles[5], imag], axis=0)
    return real.astype(BF16), imag.astype(BF16)


def spectrum(real, imag, table, sines_first=False):
    both = jnp.dot(
        jnp.concatenate([real, imag], axis=0), table, preferred_element_type=F32
    )
    rows = real.shape[0]
    of_real, of_imag = both[:rows], both[rows:]
    cosines, sines = slice(0, WAVES), slice(WAVES, 2 * WAVES)
    if sines_first:
        cosines, sines = sines, cosines
    return jnp.concatenate(
        [of_real[:, cosines] + of_imag[:, sines], of_imag[:, cosines] - of_real[:, sines]], axis=1
    )


def by_bin(values):
    tile_row = lax.broadcasted_iota(jnp.int32, (TILE, values.shape[1]), 0)
    tiles = [values[at * TILE : (at + 1) * TILE] for at in range(4)]
    four = tiles[2] + pltpu.roll(tiles[2], 4, 0)
    one = pltpu.roll(tiles[3] + pltpu.roll(tiles[3], 7, 0), 4, 0)
    rest = jnp.where(tile_row < 4, four, jnp.where(tile_row == 4, one, 0.0))
    return jnp.concatenate([tiles[0] + tiles[1], rest], axis=0)


def own_kernel(recv_ref, table_ref, cross_ref, real_ref, imag_ref, waves_ref):
    for source in range(DESTS):
        rows = slice(source * TAKEN, (source + 1) * TAKEN)
        real_ref[rows], imag_ref[rows] = parts_of(recv_ref[source])
    waves_ref[...] = spectrum(real_ref[...], imag_ref[...], table_ref[...])
    for half in range(2):
        real_at = half * OFFS
        imag_at = WAVES + half * OFFS

        def body(step, total, real_at=real_at, imag_at=imag_at, half=half):
            row = pl.multiple_of(step * TAKEN, TAKEN)
            total_real, total_imag = total
            own_real = waves_ref[pl.ds(row, TAKEN), real_at : real_at + OFFS]
            own_imag = waves_ref[pl.ds(row, TAKEN), imag_at : imag_at + OFFS]
            for block in range(SEG_BLOCKS):
                if block == SEG_BLOCKS - 1:
                    total_real = total_real + (own_real * own_real + own_imag * own_imag)
                    continue
                at = row + (block + 1) * GROUP
                next_real = waves_ref[pl.ds(at, TAKEN), real_at : real_at + OFFS]
                next_imag = waves_ref[pl.ds(at, TAKEN), imag_at : imag_at + OFFS]
                if half == 0:
                    ext_real, ext_imag = own_real + next_real, own_imag + next_imag
                else:
                    ext_real, ext_imag = own_real - next_real, own_imag - next_imag
                total_real = total_real + (own_real * ext_real + own_imag * ext_imag)
                total_imag = total_imag + (own_imag * ext_real - own_real * ext_imag)
                own_real, own_imag = next_real, next_imag
            return total_real, total_imag

        zero = jnp.zeros((TAKEN, OFFS), F32)
        total = lax.fori_loop(0, WIN_DEVICES, body, (zero, zero))
        cross_ref[:, real_at : real_at + OFFS] = total[0]
        cross_ref[:, imag_at : imag_at + OFFS] = total[1]


def own_products(received, table):
    return pl.pallas_call(
        own_kernel,
        out_shape=jax.ShapeDtypeStruct((TAKEN, 2 * WAVES), F32),
        in_specs=[pl.BlockSpec(memory_space=pltpu.VMEM)] * 2,
        out_specs=pl.BlockSpec(memory_space=pltpu.VMEM),
        scratch_shapes=[
            pltpu.VMEM((DESTS * TAKEN, OFFS), BF16),
            pltpu.VMEM((DESTS * TAKEN, OFFS), BF16),
            pltpu.VMEM((DESTS * TAKEN, 2 * WAVES), F32),
        ],
        compiler_params=pltpu.CompilerParams(vmem_limit_bytes=40 << 20),
        cost_estimate=pl.CostEstimate(
            flops=2 * 1024 * 512 * 1024, bytes_accessed=8 << 20, transcendentals=0
        ),
        name="own_products",
    )(received, table)


def image_kernel(
    ahead_ref, behind_ref, last_ref, table_ref, cross_ref, lead_ref, spread_ref, turns_ref, out_ref
):
    totals = [
        cross_ref[:, at * OFFS : (at + 1) * OFFS] for at in range(4)
    ]
    following = ahead_ref[...] + behind_ref[...]
    slots = [following[w] for w in range(WIN_DEVICES)] + [last_ref[w] for w in range(WIN_DEVICES)]
    reals, imags = zip(*[parts_of(slot) for slot in slots])
    waves = spectrum(
        jnp.concatenate(reals, axis=0), jnp.concatenate(imags, axis=0), table_ref[...], True
    )
    last = waves[GROUP:]
    waves = waves[:GROUP]
    for half in range(2):
        real_at = half * OFFS
        imag_at = WAVES + half * OFFS
        next_real = waves[:, real_at : real_at + OFFS]
        next_imag = waves[:, imag_at : imag_at + OFFS]
        own_real = last[:, real_at : real_at + OFFS]
        own_imag = last[:, imag_at : imag_at + OFFS]
        more_real = own_real * next_real + own_imag * next_imag
        more_imag = own_imag * next_real - own_real * next_imag
        more_real = jnp.sum(more_real.reshape(WIN_DEVICES, TAKEN, OFFS), axis=0)
        more_imag = jnp.sum(more_imag.reshape(WIN_DEVICES, TAKEN, OFFS), axis=0)
        sign = 1.0 if half == 0 else -1.0
        totals[half] = totals[half] + sign * more_real
        totals[2 + half] = totals[2 + half] + sign * more_imag
    cross = by_bin(jnp.concatenate(totals, axis=1))
    flat_real = jnp.sum(cross[:, :WAVES], axis=1, keepdims=True) / WAVES
    flat_imag = jnp.sum(cross[:, WAVES:], axis=1, keepdims=True) / WAVES
    cross = jnp.concatenate([cross[:, :WAVES] - flat_real, cross[:, WAVES:] - flat_imag], axis=1)
    upper = cross.astype(BF16)
    lower = (cross - upper.astype(F32)).astype(BF16)
    both = jnp.concatenate([upper, lower], axis=0)
    stack = jnp.dot(both, lead_ref[...], preferred_element_type=F32)
    stack = stack[:SLOT] + stack[SLOT:]
    lag = lax.broadcasted_iota(jnp.int32, (SLOT, 2 * OFFS), 1)
    stack = stack + jnp.where(lag == 0, flat_real, jnp.where(lag == OFFS, flat_imag, 0.0))
    real = stack[:, :OFFS]
    imag = stack[:, OFFS:]
    power = jnp.sum(real * real + imag * imag, axis=1, keepdims=True) / OFFS
    factor = 1.0 / jnp.sqrt(power + EPS)
    size = SLOT * DIGIT
    row = lax.broadcasted_iota(jnp.int32, (size, OFFS), 0)
    lane = lax.broadcasted_iota(jnp.int32, (size, OFFS), 1)
    same_digit = row // SLOT == lane // DIGIT
    same_bin = row % SLOT == lane % SLOT

    def spread(values):
        normed = values * factor
        repeated = jnp.broadcast_to(normed[None], (DIGIT, SLOT, OFFS)).reshape(size, OFFS)
        picked = jnp.where(same_digit, repeated, 0.0).astype(BF16)
        moved = jnp.dot(picked, spread_ref[...], preferred_element_type=F32)
        return jnp.where(same_bin, moved, 0.0).astype(BF16)

    turns = turns_ref[...]
    fine = [jnp.concatenate(pair, axis=1).astype(BF16) for pair in powers_of(*turn_waves(turns))]
    of_both = jnp.dot(
        jnp.concatenate([spread(real), spread(imag)], axis=0),
        jnp.concatenate(fine, axis=0),
        preferred_element_type=F32,
    )
    along = jnp.zeros((SLOT, VEL), F32)
    across = jnp.zeros((SLOT, VEL), F32)
    for at, (cosine, sine) in enumerate(powers_of(*turn_waves(turns * DIGIT))):
        one = of_both[at * SLOT : (at + 1) * SLOT]
        two = of_both[size + at * SLOT : size + (at + 1) * SLOT]
        part_real = one[:, :VEL] + two[:, VEL:]
        part_imag = two[:, :VEL] - one[:, VEL:]
        along = along + (part_real * cosine + part_imag * sine)
        across = across + (part_imag * cosine - part_real * sine)
    image = (along * along + across * across) / OFFS
    here = VEL // SEG_BLOCKS
    for block in range(SEG_BLOCKS):
        pair = image[:, block // 2 * LANES : (block // 2 + 1) * LANES]
        out_ref[block] = pair if block % 2 == 0 else jnp.roll(pair, here, axis=1)


def image_of(*arrays):
    return pl.pallas_call(
        image_kernel,
        out_shape=jax.ShapeDtypeStruct((SEG_BLOCKS, SLOT, LANES), F32),
        in_specs=[pl.BlockSpec(memory_space=pltpu.VMEM)] * 8,
        out_specs=pl.BlockSpec(memory_space=pltpu.VMEM),
        compiler_params=pltpu.CompilerParams(vmem_limit_bytes=40 << 20),
        cost_estimate=pl.CostEstimate(
            flops=2 * 700 * 512 * 1024, bytes_accessed=6 << 20, transcendentals=0
        ),
        name="image",
    )(*arrays)


def gather(parts, table):
    rows = parts.reshape(SEG_BLOCKS * SLOT, LANES)
    gathered = lax.dot_general(
        rows,
        table,
        (((0,), (0,)), ((), ())),
        precision=lax.Precision.HIGHEST,
        preferred_element_type=F32,
    )
    return gathered[: VEL // SEG_BLOCKS]


def local(samples_data, coupling):
    whitened = whiten(samples_data, coupling[None, :], jnp.asarray(time_table()))
    segments = lax.axis_size("seg")
    middle = segments // 2
    place = (lax.axis_index("blk"), lax.axis_index("win"))
    table = jnp.asarray(forward_table())

    def exchange(values):
        return lax.all_to_all(values, ("blk", "win"), 0, 0, tiled=True)

    before = lax.axis_index("seg") < middle
    received = lax.cond(before, lambda values: values, exchange, whitened)
    behind = lax.ppermute(
        received[:WIN_DEVICES], "seg", [(s, s - 1) for s in range(middle, segments)]
    )
    nothing = lax.optimization_barrier(jnp.zeros((TAKEN, 2 * WAVES), F32))
    received, cross, table = lax.cond(
        before,
        lambda values, same, table: (exchange(values), same, table),
        lambda values, _, table: (values, own_products(values, table), table),
        received,
        nothing,
        table,
    )
    behind, received, cross, table = lax.optimization_barrier((behind, received, cross, table))
    ahead = lax.ppermute(received[:WIN_DEVICES], "seg", [(s, s - 1) for s in range(1, middle)])
    cross = lax.cond(
        before,
        lambda values, _, table: own_products(values, table),
        lambda _, same, table: same,
        received,
        cross,
        table,
    )
    images = image_of(
        ahead,
        behind,
        received[-WIN_DEVICES:],
        jnp.asarray(forward_table(sines_first=True)),
        cross,
        jnp.asarray(inverse_table()),
        jnp.asarray(spread_table()),
        turns_of(*place),
    )
    images = lax.all_to_all(images, "blk", 0, 0, tiled=True)
    return gather(images, jnp.asarray(gather_table()))


def solution(mesh):
    segments = mesh.shape["fibre"] // SEG_BLOCKS
    inner = Mesh(
        mesh.devices.reshape(segments, SEG_BLOCKS, mesh.shape["win"]), ("seg", "blk", "win")
    )
    placed = (P("win", None, ("seg", "blk")), P(("seg", "blk")))
    return jax.shard_map(
        local, mesh=inner, in_specs=placed, out_specs=P(("seg", "blk"), "win"), check_vma=False
    )
```

```python
import math

import jax
import jax.numpy as jnp
import ml_dtypes
import numpy as np
from jax import lax
from jax.experimental import pallas as pl
from jax.experimental.pallas import tpu as pltpu
from jax.sharding import Mesh, PartitionSpec as P

SAMPLES = 2000
FREQS = 400
OFFS = 256
VEL = 512
SEG_BLOCKS = 8
EPS = 1e-06

WIN_DEVICES = 4
DESTS = SEG_BLOCKS * WIN_DEVICES
CHUNK = FREQS // WIN_DEVICES
FIRST_BIN = [0, 13, 25, 38, 50, 63, 75, 88, CHUNK]
SLOT = 16
TILE = 8
SENT = 13 * TILE
TAKEN = 4 * TILE
LOCAL_WINDOWS = 2
DIGIT = 16
ROWS = SEG_BLOCKS * 13 * TILE
LANES = 128
STEP = 256
STEPS = 4
HALF = SAMPLES // 2
BF16 = jnp.bfloat16
F32 = jnp.float32


def bins_of(block, window_device):
    rows = np.arange(SLOT)
    within = FIRST_BIN[block] + rows
    return np.where(within < FIRST_BIN[block + 1], window_device * CHUNK + within, -1)


def table_rows():
    bins, parts = [], []
    for block in range(SEG_BLOCKS):
        dests = [bins_of(block, window_device) for window_device in range(WIN_DEVICES)]
        rows = []
        for dest in dests:
            for first, last in ((0, 8), (8, 12)):
                for part in (0, 1):
                    rows += [(dest[r], part) for r in range(first, last)]
        rows += [(dest[12], part) for part in (0, 1) for dest in dests]
        for at, part in rows:
            bins.append(at)
            parts.append(part)
    return np.array(bins), np.array(parts)


def time_table():
    bins, parts = table_rows()
    times = np.arange(STEP * STEPS, dtype=np.int64)
    turns = ((bins[:, None] + 1) * times[None, :]) % SAMPLES
    angle = np.float32(2.0 * math.pi / SAMPLES) * turns.astype(np.float32)
    valid = (bins >= 0)[:, None] & (times < SAMPLES // 2)[None, :]
    waves = np.where(parts[:, None] == 0, np.cos(angle), -np.sin(angle))
    table = np.where(valid, waves, 0.0).reshape(ROWS, STEPS, STEP)
    return table.transpose(1, 0, 2).astype(np.float32).astype(ml_dtypes.bfloat16)


def wave_order():
    return np.concatenate([np.arange(0, 2 * OFFS, 2), np.arange(1, 2 * OFFS, 2)])


def forward_table(sines_first=False):
    rows = np.arange(OFFS)
    angle = 2.0 * np.pi / (2 * OFFS) * ((rows[:, None] * wave_order()[None, :]) % (2 * OFFS))
    halves = [np.cos(angle), np.sin(angle)]
    table = np.concatenate(halves[::-1] if sines_first else halves, axis=1)
    return table.astype(np.float32).astype(ml_dtypes.bfloat16)


def inverse_table():
    lags = np.arange(OFFS)
    angle = 2.0 * np.pi / (2 * OFFS) * ((wave_order()[:, None] * lags[None, :]) % (2 * OFFS))
    table = np.concatenate([np.cos(angle), np.sin(angle)], axis=1) / (2 * OFFS)
    return table.astype(np.float32).astype(ml_dtypes.bfloat16)


def spread_table():
    index = np.arange(OFFS)
    same = (index[:, None] % DIGIT) == (index[None, :] // SLOT)
    return same.astype(ml_dtypes.bfloat16)


def gather_table():
    table = np.zeros((SEG_BLOCKS * SLOT, CHUNK), np.float32)
    for block in range(SEG_BLOCKS):
        for row in range(FIRST_BIN[block + 1] - FIRST_BIN[block]):
            table[block * SLOT + row, FIRST_BIN[block] + row] = 1.0
    return table


def turn_waves(turns):
    rest = turns - jnp.floor(turns + 0.5)
    half = rest * math.pi
    square = half * half
    sine = half * (
        1.0
        + square
        * (
            -1.0 / 6
            + square
            * (1.0 / 120 + square * (-1.0 / 5040 + square * (1.0 / 362880 - square / 39916800)))
        )
    )
    cosine = 1.0 + square * (
        -0.5
        + square
        * (
            1.0 / 24
            + square
            * (
                -1.0 / 720
                + square * (1.0 / 40320 + square * (-1.0 / 3628800 + square / 479001600))
            )
        )
    )
    return 1.0 - 2.0 * sine * sine, 2.0 * sine * cosine


def turns_of(block, window_device):
    speeds = jnp.arange(VEL, dtype=jnp.int32)
    speed = 150.0 + 1350.0 * speeds.astype(F32) / (VEL - 1)
    slowness = (200.0 * 8.0 / SAMPLES / speed)[None, :]
    first = window_device * CHUNK + (25 * block + 1) // 2 + 1
    return (first + jnp.arange(SLOT, dtype=jnp.int32)).astype(F32)[:, None] * slowness


def powers_of(cosine, sine):
    now = (jnp.ones_like(cosine), jnp.zeros_like(sine))
    waves = [now]
    for _ in range(DIGIT - 1):
        now = (now[0] * cosine - now[1] * sine, now[1] * cosine + now[0] * sine)
        waves.append(now)
    return waves


def whiten_kernel(
    samples_hbm,
    table_hbm,
    weights_hbm,
    out_ref,
    early_ref,
    late_ref,
    table_ref,
    weights_ref,
    raw_ref,
    in_sems,
):
    weights_copy = pltpu.make_async_copy(weights_hbm, weights_ref, in_sems.at[3 * STEPS])
    copies = []
    for step in range(STEPS):
        early = STEP
        late_at = 992 + step * STEP
        late = min(STEP + 16, SAMPLES - late_at)
        copies.append(
            [
                pltpu.make_async_copy(
                    table_hbm.at[step], table_ref.at[step], in_sems.at[3 * step]
                ),
                pltpu.make_async_copy(
                    samples_hbm.at[:, pl.ds(step * STEP, early), :],
                    early_ref.at[step, :, pl.ds(0, early), :],
                    in_sems.at[3 * step + 1],
                ),
                pltpu.make_async_copy(
                    samples_hbm.at[:, pl.ds(late_at, late), :],
                    late_ref.at[step, :, pl.ds(0, late), :],
                    in_sems.at[3 * step + 2],
                ),
            ]
        )
        for copy in copies[-1]:
            copy.start()
    weights_copy.start()

    row = lax.broadcasted_iota(jnp.int32, (ROWS // SEG_BLOCKS, STEP), 0)
    odd = jnp.where((row % 2 == 0) | (row >= 12 * TILE), -1.0, 1.0)
    sign = jnp.concatenate(
        [odd if FIRST_BIN[block] % 2 == 0 else -odd for block in range(SEG_BLOCKS)], axis=0
    ).astype(BF16)
    tile_row = lax.broadcasted_iota(jnp.int32, (TILE, OFFS), 0)
    upper_half = tile_row < 4
    missing = HALF - (STEPS - 1) * STEP + 8
    late_ref[STEPS - 1, :, missing:, :] = jnp.zeros(
        (LOCAL_WINDOWS, STEP + 16 - missing, OFFS), BF16
    )
    powers = None
    for step in range(STEPS):
        for copy in copies[step]:
            copy.wait()
        table = table_ref[step]
        turned = table * sign
        pair = jnp.concatenate([table, turned], axis=1)
        samples = jnp.concatenate(
            [
                jnp.concatenate(
                    [early_ref[step, w], late_ref[step, w, 8 : 8 + STEP, :]], axis=0
                )
                for w in range(LOCAL_WINDOWS)
            ],
            axis=1,
        )
        raw = jnp.dot(pair, samples, preferred_element_type=F32)
        if step > 0:
            raw = raw + raw_ref[...]
        raw_ref[...] = raw
        if step == STEPS - 1:
            powers = jnp.sum((raw * raw).reshape(ROWS // 8, 8, LOCAL_WINDOWS * OFFS), axis=0)

    weights_copy.wait()
    factors = []
    for w in range(LOCAL_WINDOWS):
        power = jnp.sum(powers[:, w * OFFS : (w + 1) * OFFS], axis=0, keepdims=True) / FREQS
        factors.append(weights_ref[...] / jnp.sqrt(power + EPS))
    for block in range(SEG_BLOCKS):
        rows = slice(block * 13 * TILE, (block + 1) * 13 * TILE)
        values = [
            raw_ref[rows, w * OFFS : (w + 1) * OFFS] * factors[w]
            for w in range(LOCAL_WINDOWS)
        ]
        final = [value[12 * TILE :] for value in values]
        for dest in range(WIN_DEVICES):
            one, two = [
                value[3 * dest * TILE : 3 * (dest + 1) * TILE] for value in values
            ]
            ends = [one[2 * TILE :], two[2 * TILE :]]
            six = jnp.concatenate(
                [
                    one[: 2 * TILE],
                    two[: 2 * TILE],
                    jnp.where(upper_half, ends[0], pltpu.roll(ends[1], 4, 0)),
                    jnp.where(upper_half, pltpu.roll(ends[0], 4, 0), ends[1]),
                ],
                axis=0,
            )
            moved = [
                pltpu.roll(final[at % 2], (at - at // 2 * 4 - dest) % TILE, 0)
                for at in range(4)
            ]
            mixed = moved[3]
            for at in range(3):
                mixed = jnp.where(tile_row == at, moved[at], mixed)
            mixed = jnp.where(
                upper_half[:, :LANES],
                mixed[:, :LANES],
                pltpu.roll(mixed[:, LANES:], 4, 0),
            )
            out_ref[block * WIN_DEVICES + dest] = jnp.concatenate(
                [six[:, :LANES], six[:, LANES:], mixed], axis=0
            ).astype(BF16)


def whiten(samples, weights, table):
    return pl.pallas_call(
        whiten_kernel,
        in_specs=[pl.BlockSpec(memory_space=pl.ANY)] * 3,
        out_specs=pl.BlockSpec(memory_space=pltpu.VMEM),
        out_shape=jax.ShapeDtypeStruct((DESTS, SENT, LANES), BF16),
        scratch_shapes=[
            pltpu.VMEM((STEPS, LOCAL_WINDOWS, STEP, OFFS), BF16),
            pltpu.VMEM((STEPS, LOCAL_WINDOWS, STEP + 16, OFFS), BF16),
            pltpu.VMEM((STEPS, ROWS, STEP), BF16),
            pltpu.VMEM((1, OFFS), F32),
            pltpu.VMEM((ROWS, LOCAL_WINDOWS * OFFS), F32),
            pltpu.SemaphoreType.DMA((3 * STEPS + 1,)),
        ],
        compiler_params=pltpu.CompilerParams(vmem_limit_bytes=62 << 20),
        cost_estimate=pl.CostEstimate(
            flops=2 * ROWS * SAMPLES * 512, bytes_accessed=5 << 20, transcendentals=0
        ),
        name="whiten",
    )(samples, table, weights)


GROUP = WIN_DEVICES * TAKEN
WAVES = 2 * OFFS


def parts_of(slot):
    values = slot.astype(F32)
    six = jnp.concatenate([values[: 6 * TILE], values[6 * TILE : 12 * TILE]], axis=1)
    tiles = [six[at * TILE : (at + 1) * TILE] for at in range(6)]
    mixed = values[12 * TILE :]
    real = jnp.concatenate([mixed, pltpu.roll(mixed, 4, 0)], axis=1)
    imag = jnp.concatenate([pltpu.roll(mixed, 6, 0), pltpu.roll(mixed, 2, 0)], axis=1)
    real = jnp.concatenate([tiles[0], tiles[2], tiles[4], real], axis=0)
    imag = jnp.concatenate([tiles[1], tiles[3], tiles[5], imag], axis=0)
    return real.astype(BF16), imag.astype(BF16)


def spectrum(real, imag, table, sines_first=False):
    both = jnp.dot(
        jnp.concatenate([real, imag], axis=0), table, preferred_element_type=F32
    )
    rows = real.shape[0]
    of_real, of_imag = both[:rows], both[rows:]
    cosines, sines = slice(0, WAVES), slice(WAVES, 2 * WAVES)
    if sines_first:
        cosines, sines = sines, cosines
    return jnp.concatenate(
        [of_real[:, cosines] + of_imag[:, sines], of_imag[:, cosines] - of_real[:, sines]], axis=1
    )


def by_bin(values):
    tile_row = lax.broadcasted_iota(jnp.int32, (TILE, values.shape[1]), 0)
    tiles = [values[at * TILE : (at + 1) * TILE] for at in range(4)]
    four = tiles[2] + pltpu.roll(tiles[2], 4, 0)
    one = pltpu.roll(tiles[3] + pltpu.roll(tiles[3], 7, 0), 4, 0)
    rest = jnp.where(tile_row < 4, four, jnp.where(tile_row == 4, one, 0.0))
    return jnp.concatenate([tiles[0] + tiles[1], rest], axis=0)


def own_kernel(recv_ref, table_ref, cross_ref, real_ref, imag_ref, waves_ref):
    for source in range(DESTS):
        rows = slice(source * TAKEN, (source + 1) * TAKEN)
        real_ref[rows], imag_ref[rows] = parts_of(recv_ref[source])
    waves_ref[...] = spectrum(real_ref[...], imag_ref[...], table_ref[...])
    for half in range(2):
        real_at = half * OFFS
        imag_at = WAVES + half * OFFS

        def body(step, total, real_at=real_at, imag_at=imag_at, half=half):
            row = pl.multiple_of(step * TAKEN, TAKEN)
            total_real, total_imag = total
            own_real = waves_ref[pl.ds(row, TAKEN), real_at : real_at + OFFS]
            own_imag = waves_ref[pl.ds(row, TAKEN), imag_at : imag_at + OFFS]
            for block in range(SEG_BLOCKS):
                if block == SEG_BLOCKS - 1:
                    total_real = total_real + (own_real * own_real + own_imag * own_imag)
                    continue
                at = row + (block + 1) * GROUP
                next_real = waves_ref[pl.ds(at, TAKEN), real_at : real_at + OFFS]
                next_imag = waves_ref[pl.ds(at, TAKEN), imag_at : imag_at + OFFS]
                if half == 0:
                    ext_real, ext_imag = own_real + next_real, own_imag + next_imag
                else:
                    ext_real, ext_imag = own_real - next_real, own_imag - next_imag
                total_real = total_real + (own_real * ext_real + own_imag * ext_imag)
                total_imag = total_imag + (own_imag * ext_real - own_real * ext_imag)
                own_real, own_imag = next_real, next_imag
            return total_real, total_imag

        zero = jnp.zeros((TAKEN, OFFS), F32)
        total = lax.fori_loop(0, WIN_DEVICES, body, (zero, zero))
        cross_ref[:, real_at : real_at + OFFS] = total[0]
        cross_ref[:, imag_at : imag_at + OFFS] = total[1]


def own_products(received, table):
    return pl.pallas_call(
        own_kernel,
        out_shape=jax.ShapeDtypeStruct((TAKEN, 2 * WAVES), F32),
        in_specs=[pl.BlockSpec(memory_space=pltpu.VMEM)] * 2,
        out_specs=pl.BlockSpec(memory_space=pltpu.VMEM),
        scratch_shapes=[
            pltpu.VMEM((DESTS * TAKEN, OFFS), BF16),
            pltpu.VMEM((DESTS * TAKEN, OFFS), BF16),
            pltpu.VMEM((DESTS * TAKEN, 2 * WAVES), F32),
        ],
        compiler_params=pltpu.CompilerParams(vmem_limit_bytes=40 << 20),
        cost_estimate=pl.CostEstimate(
            flops=2 * 1024 * 512 * 1024, bytes_accessed=8 << 20, transcendentals=0
        ),
        name="own_products",
    )(received, table)


def image_kernel(
    ahead_ref, behind_ref, last_ref, table_ref, cross_ref, lead_ref, spread_ref, turns_ref, out_ref
):
    totals = [
        cross_ref[:, at * OFFS : (at + 1) * OFFS] for at in range(4)
    ]
    following = ahead_ref[...] + behind_ref[...]
    slots = [following[w] for w in range(WIN_DEVICES)] + [last_ref[w] for w in range(WIN_DEVICES)]
    reals, imags = zip(*[parts_of(slot) for slot in slots])
    waves = spectrum(
        jnp.concatenate(reals, axis=0), jnp.concatenate(imags, axis=0), table_ref[...], True
    )
    last = waves[GROUP:]
    waves = waves[:GROUP]
    for half in range(2):
        real_at = half * OFFS
        imag_at = WAVES + half * OFFS
        next_real = waves[:, real_at : real_at + OFFS]
        next_imag = waves[:, imag_at : imag_at + OFFS]
        own_real = last[:, real_at : real_at + OFFS]
        own_imag = last[:, imag_at : imag_at + OFFS]
        more_real = own_real * next_real + own_imag * next_imag
        more_imag = own_imag * next_real - own_real * next_imag
        more_real = jnp.sum(more_real.reshape(WIN_DEVICES, TAKEN, OFFS), axis=0)
        more_imag = jnp.sum(more_imag.reshape(WIN_DEVICES, TAKEN, OFFS), axis=0)
        sign = 1.0 if half == 0 else -1.0
        totals[half] = totals[half] + sign * more_real
        totals[2 + half] = totals[2 + half] + sign * more_imag
    cross = by_bin(jnp.concatenate(totals, axis=1))
    flat_real = jnp.sum(cross[:, :WAVES], axis=1, keepdims=True) / WAVES
    flat_imag = jnp.sum(cross[:, WAVES:], axis=1, keepdims=True) / WAVES
    cross = jnp.concatenate([cross[:, :WAVES] - flat_real, cross[:, WAVES:] - flat_imag], axis=0)
    upper = cross.astype(BF16)
    lower = (cross - upper.astype(F32)).astype(BF16)
    both = jnp.dot(
        jnp.concatenate([upper, lower], axis=0), lead_ref[...], preferred_element_type=F32
    )
    both = both[: 2 * SLOT] + both[2 * SLOT :]
    of_real, of_imag = both[:SLOT], both[SLOT:]
    lag = lax.broadcasted_iota(jnp.int32, (SLOT, OFFS), 1)
    real = of_real[:, :OFFS] + of_imag[:, OFFS:] + jnp.where(lag == 0, flat_real, 0.0)
    imag = of_imag[:, :OFFS] - of_real[:, OFFS:] + jnp.where(lag == 0, flat_imag, 0.0)
    power = jnp.sum(real * real + imag * imag, axis=1, keepdims=True) / OFFS
    factor = 1.0 / jnp.sqrt(power + EPS)
    size = SLOT * DIGIT
    row = lax.broadcasted_iota(jnp.int32, (size, OFFS), 0)
    lane = lax.broadcasted_iota(jnp.int32, (size, OFFS), 1)
    same_digit = row // SLOT == lane // DIGIT
    same_bin = row % SLOT == lane % SLOT

    def repeated(values):
        normed = values * factor
        return jnp.broadcast_to(normed[None], (DIGIT, SLOT, OFFS)).reshape(size, OFFS)

    picked = jnp.concatenate(
        [jnp.where(same_digit, repeated(part), 0.0).astype(BF16) for part in (real, imag)], axis=0
    )
    moved = jnp.dot(picked, spread_ref[...], preferred_element_type=F32)
    moved = jnp.concatenate(
        [jnp.where(same_bin, moved[at * size : (at + 1) * size], 0.0) for at in range(2)], axis=0
    ).astype(BF16)
    turns = turns_ref[...]
    fine = [jnp.concatenate(pair, axis=1).astype(BF16) for pair in powers_of(*turn_waves(turns))]
    of_both = jnp.dot(
        moved, jnp.concatenate(fine, axis=0), preferred_element_type=F32
    )
    along = jnp.zeros((SLOT, VEL), F32)
    across = jnp.zeros((SLOT, VEL), F32)
    for at, (cosine, sine) in enumerate(powers_of(*turn_waves(turns * DIGIT))):
        one = of_both[at * SLOT : (at + 1) * SLOT]
        two = of_both[size + at * SLOT : size + (at + 1) * SLOT]
        part_real = one[:, :VEL] + two[:, VEL:]
        part_imag = two[:, :VEL] - one[:, VEL:]
        along = along + (part_real * cosine + part_imag * sine)
        across = across + (part_imag * cosine - part_real * sine)
    image = (along * along + across * across) / OFFS
    here = VEL // SEG_BLOCKS
    for block in range(SEG_BLOCKS):
        pair = image[:, block // 2 * LANES : (block // 2 + 1) * LANES]
        out_ref[block] = pair if block % 2 == 0 else jnp.roll(pair, here, axis=1)


def image_of(*arrays):
    return pl.pallas_call(
        image_kernel,
        out_shape=jax.ShapeDtypeStruct((SEG_BLOCKS, SLOT, LANES), F32),
        in_specs=[pl.BlockSpec(memory_space=pltpu.VMEM)] * 8,
        out_specs=pl.BlockSpec(memory_space=pltpu.VMEM),
        compiler_params=pltpu.CompilerParams(vmem_limit_bytes=40 << 20),
        cost_estimate=pl.CostEstimate(
            flops=2 * 700 * 512 * 1024, bytes_accessed=6 << 20, transcendentals=0
        ),
        name="image",
    )(*arrays)


def gather(parts, table):
    rows = parts.reshape(SEG_BLOCKS * SLOT, LANES)
    gathered = lax.dot_general(
        rows,
        table,
        (((0,), (0,)), ((), ())),
        precision=lax.Precision.HIGHEST,
        preferred_element_type=F32,
    )
    return gathered[: VEL // SEG_BLOCKS]


def local(samples_data, coupling):
    whitened = whiten(samples_data, coupling[None, :], jnp.asarray(time_table()))
    segments = lax.axis_size("seg")
    middle = segments // 2
    place = (lax.axis_index("blk"), lax.axis_index("win"))
    table = jnp.asarray(forward_table())

    def exchange(values):
        return lax.all_to_all(values, ("blk", "win"), 0, 0, tiled=True)

    before = lax.axis_index("seg") < middle
    received = lax.cond(before, lambda values: values, exchange, whitened)
    behind = lax.ppermute(
        received[:WIN_DEVICES], "seg", [(s, s - 1) for s in range(middle, segments)]
    )
    nothing = lax.optimization_barrier(jnp.zeros((TAKEN, 2 * WAVES), F32))
    received, cross, table = lax.cond(
        before,
        lambda values, same, table: (exchange(values), same, table),
        lambda values, _, table: (values, own_products(values, table), table),
        received,
        nothing,
        table,
    )
    behind, received, cross, table = lax.optimization_barrier((behind, received, cross, table))
    ahead = lax.ppermute(received[:WIN_DEVICES], "seg", [(s, s - 1) for s in range(1, middle)])
    cross = lax.cond(
        before,
        lambda values, _, table: own_products(values, table),
        lambda _, same, table: same,
        received,
        cross,
        table,
    )
    images = image_of(
        ahead,
        behind,
        received[-WIN_DEVICES:],
        jnp.asarray(forward_table(sines_first=True)),
        cross,
        jnp.asarray(inverse_table()),
        jnp.asarray(spread_table()),
        turns_of(*place),
    )
    images = lax.all_to_all(images, "blk", 0, 0, tiled=True)
    return gather(images, jnp.asarray(gather_table()))


def solution(mesh):
    segments = mesh.shape["fibre"] // SEG_BLOCKS
    inner = Mesh(
        mesh.devices.reshape(segments, SEG_BLOCKS, mesh.shape["win"]), ("seg", "blk", "win")
    )
    placed = (P("win", None, ("seg", "blk")), P(("seg", "blk")))
    return jax.shard_map(
        local, mesh=inner, in_specs=placed, out_specs=P(("seg", "blk"), "win"), check_vma=False
    )
```

```python
import math

import jax
import jax.numpy as jnp
import ml_dtypes
import numpy as np
from jax import lax
from jax.experimental import pallas as pl
from jax.experimental.pallas import tpu as pltpu
from jax.sharding import Mesh, PartitionSpec as P

SAMPLES = 2000
FREQS = 400
OFFS = 256
VEL = 512
SEG_BLOCKS = 8
EPS = 1e-06

WIN_DEVICES = 4
DESTS = SEG_BLOCKS * WIN_DEVICES
CHUNK = FREQS // WIN_DEVICES
FIRST_BIN = [0, 13, 25, 38, 50, 63, 75, 88, CHUNK]
SLOT = 16
TILE = 8
SENT = 13 * TILE
TAKEN = 4 * TILE
LOCAL_WINDOWS = 2
DIGIT = 16
ROWS = SEG_BLOCKS * 13 * TILE
LANES = 128
STEP = 256
STEPS = 4
HALF = SAMPLES // 2
BF16 = jnp.bfloat16
F32 = jnp.float32


def bins_of(block, window_device):
    rows = np.arange(SLOT)
    within = FIRST_BIN[block] + rows
    return np.where(within < FIRST_BIN[block + 1], window_device * CHUNK + within, -1)


def table_rows():
    bins, parts = [], []
    for block in range(SEG_BLOCKS):
        dests = [bins_of(block, window_device) for window_device in range(WIN_DEVICES)]
        rows = []
        for dest in dests:
            for first, last in ((0, 8), (8, 12)):
                for part in (0, 1):
                    rows += [(dest[r], part) for r in range(first, last)]
        rows += [(dest[12], part) for part in (0, 1) for dest in dests]
        for at, part in rows:
            bins.append(at)
            parts.append(part)
    return np.array(bins), np.array(parts)


def time_table():
    bins, parts = table_rows()
    times = np.arange(STEP * STEPS, dtype=np.int64)
    turns = ((bins[:, None] + 1) * times[None, :]) % SAMPLES
    angle = np.float32(2.0 * math.pi / SAMPLES) * turns.astype(np.float32)
    valid = (bins >= 0)[:, None] & (times < SAMPLES // 2)[None, :]
    waves = np.where(parts[:, None] == 0, np.cos(angle), -np.sin(angle))
    table = np.where(valid, waves, 0.0).reshape(ROWS, STEPS, STEP)
    return table.transpose(1, 0, 2).astype(np.float32).astype(ml_dtypes.bfloat16)


def wave_order():
    return np.concatenate([np.arange(0, 2 * OFFS, 2), np.arange(1, 2 * OFFS, 2)])


def forward_table(sines_first=False):
    rows = np.arange(OFFS)
    angle = 2.0 * np.pi / (2 * OFFS) * ((rows[:, None] * wave_order()[None, :]) % (2 * OFFS))
    halves = [np.cos(angle), np.sin(angle)]
    table = np.concatenate(halves[::-1] if sines_first else halves, axis=1)
    return table.astype(np.float32).astype(ml_dtypes.bfloat16)


def inverse_table():
    lags = np.arange(OFFS)
    angle = 2.0 * np.pi / (2 * OFFS) * ((wave_order()[:, None] * lags[None, :]) % (2 * OFFS))
    table = np.concatenate([np.cos(angle), np.sin(angle)], axis=1) / (2 * OFFS)
    return table.astype(np.float32).astype(ml_dtypes.bfloat16)


def spread_table():
    index = np.arange(OFFS)
    same = (index[:, None] % DIGIT) == (index[None, :] // SLOT)
    return same.astype(ml_dtypes.bfloat16)


def gather_table():
    table = np.zeros((SEG_BLOCKS * SLOT, CHUNK), np.float32)
    for block in range(SEG_BLOCKS):
        for row in range(FIRST_BIN[block + 1] - FIRST_BIN[block]):
            table[block * SLOT + row, FIRST_BIN[block] + row] = 1.0
    return table


def turn_waves(turns):
    rest = turns - jnp.floor(turns + 0.5)
    half = rest * math.pi
    square = half * half
    sine = half * (
        1.0
        + square
        * (
            -1.0 / 6
            + square
            * (1.0 / 120 + square * (-1.0 / 5040 + square * (1.0 / 362880 - square / 39916800)))
        )
    )
    cosine = 1.0 + square * (
        -0.5
        + square
        * (
            1.0 / 24
            + square
            * (
                -1.0 / 720
                + square * (1.0 / 40320 + square * (-1.0 / 3628800 + square / 479001600))
            )
        )
    )
    return 1.0 - 2.0 * sine * sine, 2.0 * sine * cosine


def turns_of(block, window_device):
    speeds = jnp.arange(VEL, dtype=jnp.int32)
    speed = 150.0 + 1350.0 * speeds.astype(F32) / (VEL - 1)
    slowness = (200.0 * 8.0 / SAMPLES / speed)[None, :]
    first = window_device * CHUNK + (25 * block + 1) // 2 + 1
    return (first + jnp.arange(SLOT, dtype=jnp.int32)).astype(F32)[:, None] * slowness


def powers_of(cosine, sine):
    waves = [(jnp.ones_like(cosine), jnp.zeros_like(sine)), (cosine, sine)]
    for power in range(2, DIGIT):
        one, two = waves[power // 2], waves[power - power // 2]
        waves.append((one[0] * two[0] - one[1] * two[1], one[1] * two[0] + one[0] * two[1]))
    return waves


def whiten_kernel(
    samples_hbm,
    table_hbm,
    weights_hbm,
    out_ref,
    early_ref,
    late_ref,
    table_ref,
    weights_ref,
    raw_ref,
    in_sems,
):
    weights_copy = pltpu.make_async_copy(weights_hbm, weights_ref, in_sems.at[3 * STEPS])
    copies = []
    for step in range(STEPS):
        early = STEP
        late_at = 992 + step * STEP
        late = min(STEP + 16, SAMPLES - late_at)
        copies.append(
            [
                pltpu.make_async_copy(
                    table_hbm.at[step], table_ref.at[step], in_sems.at[3 * step]
                ),
                pltpu.make_async_copy(
                    samples_hbm.at[:, pl.ds(step * STEP, early), :],
                    early_ref.at[step, :, pl.ds(0, early), :],
                    in_sems.at[3 * step + 1],
                ),
                pltpu.make_async_copy(
                    samples_hbm.at[:, pl.ds(late_at, late), :],
                    late_ref.at[step, :, pl.ds(0, late), :],
                    in_sems.at[3 * step + 2],
                ),
            ]
        )
        for copy in copies[-1]:
            copy.start()
    weights_copy.start()

    row = lax.broadcasted_iota(jnp.int32, (ROWS // SEG_BLOCKS, STEP), 0)
    odd = jnp.where((row % 2 == 0) | (row >= 12 * TILE), -1.0, 1.0)
    sign = jnp.concatenate(
        [odd if FIRST_BIN[block] % 2 == 0 else -odd for block in range(SEG_BLOCKS)], axis=0
    ).astype(BF16)
    tile_row = lax.broadcasted_iota(jnp.int32, (TILE, OFFS), 0)
    upper_half = tile_row < 4
    missing = HALF - (STEPS - 1) * STEP + 8
    late_ref[STEPS - 1, :, missing:, :] = jnp.zeros(
        (LOCAL_WINDOWS, STEP + 16 - missing, OFFS), BF16
    )
    powers = None
    for step in range(STEPS):
        for copy in copies[step]:
            copy.wait()
        table = table_ref[step]
        turned = table * sign
        pair = jnp.concatenate([table, turned], axis=1)
        samples = jnp.concatenate(
            [
                jnp.concatenate(
                    [early_ref[step, w], late_ref[step, w, 8 : 8 + STEP, :]], axis=0
                )
                for w in range(LOCAL_WINDOWS)
            ],
            axis=1,
        )
        raw = jnp.dot(pair, samples, preferred_element_type=F32)
        if step > 0:
            raw = raw + raw_ref[...]
        raw_ref[...] = raw
        if step == STEPS - 1:
            powers = jnp.sum((raw * raw).reshape(ROWS // 8, 8, LOCAL_WINDOWS * OFFS), axis=0)

    weights_copy.wait()
    factors = []
    for w in range(LOCAL_WINDOWS):
        power = jnp.sum(powers[:, w * OFFS : (w + 1) * OFFS], axis=0, keepdims=True) / FREQS
        factors.append(weights_ref[...] / jnp.sqrt(power + EPS))
    for block in range(SEG_BLOCKS):
        rows = slice(block * 13 * TILE, (block + 1) * 13 * TILE)
        values = [
            raw_ref[rows, w * OFFS : (w + 1) * OFFS] * factors[w]
            for w in range(LOCAL_WINDOWS)
        ]
        final = [value[12 * TILE :] for value in values]
        for dest in range(WIN_DEVICES):
            one, two = [
                value[3 * dest * TILE : 3 * (dest + 1) * TILE] for value in values
            ]
            ends = [one[2 * TILE :], two[2 * TILE :]]
            six = jnp.concatenate(
                [
                    one[: 2 * TILE],
                    two[: 2 * TILE],
                    jnp.where(upper_half, ends[0], pltpu.roll(ends[1], 4, 0)),
                    jnp.where(upper_half, pltpu.roll(ends[0], 4, 0), ends[1]),
                ],
                axis=0,
            )
            moved = [
                pltpu.roll(final[at % 2], (at - at // 2 * 4 - dest) % TILE, 0)
                for at in range(4)
            ]
            mixed = moved[3]
            for at in range(3):
                mixed = jnp.where(tile_row == at, moved[at], mixed)
            mixed = jnp.where(
                upper_half[:, :LANES],
                mixed[:, :LANES],
                pltpu.roll(mixed[:, LANES:], 4, 0),
            )
            out_ref[block * WIN_DEVICES + dest] = jnp.concatenate(
                [six[:, :LANES], six[:, LANES:], mixed], axis=0
            ).astype(BF16)


def whiten(samples, weights, table):
    return pl.pallas_call(
        whiten_kernel,
        in_specs=[pl.BlockSpec(memory_space=pl.ANY)] * 3,
        out_specs=pl.BlockSpec(memory_space=pltpu.VMEM),
        out_shape=jax.ShapeDtypeStruct((DESTS, SENT, LANES), BF16),
        scratch_shapes=[
            pltpu.VMEM((STEPS, LOCAL_WINDOWS, STEP, OFFS), BF16),
            pltpu.VMEM((STEPS, LOCAL_WINDOWS, STEP + 16, OFFS), BF16),
            pltpu.VMEM((STEPS, ROWS, STEP), BF16),
            pltpu.VMEM((1, OFFS), F32),
            pltpu.VMEM((ROWS, LOCAL_WINDOWS * OFFS), F32),
            pltpu.SemaphoreType.DMA((3 * STEPS + 1,)),
        ],
        compiler_params=pltpu.CompilerParams(vmem_limit_bytes=62 << 20),
        cost_estimate=pl.CostEstimate(
            flops=2 * ROWS * SAMPLES * 512, bytes_accessed=5 << 20, transcendentals=0
        ),
        name="whiten",
    )(samples, table, weights)


GROUP = WIN_DEVICES * TAKEN
WAVES = 2 * OFFS


def parts_of(slot):
    values = slot.astype(F32)
    six = jnp.concatenate([values[: 6 * TILE], values[6 * TILE : 12 * TILE]], axis=1)
    tiles = [six[at * TILE : (at + 1) * TILE] for at in range(6)]
    mixed = values[12 * TILE :]
    real = jnp.concatenate([mixed, pltpu.roll(mixed, 4, 0)], axis=1)
    imag = jnp.concatenate([pltpu.roll(mixed, 6, 0), pltpu.roll(mixed, 2, 0)], axis=1)
    real = jnp.concatenate([tiles[0], tiles[2], tiles[4], real], axis=0)
    imag = jnp.concatenate([tiles[1], tiles[3], tiles[5], imag], axis=0)
    return real.astype(BF16), imag.astype(BF16)


def spectrum(real, imag, table, sines_first=False):
    both = jnp.dot(
        jnp.concatenate([real, imag], axis=0), table, preferred_element_type=F32
    )
    rows = real.shape[0]
    of_real, of_imag = both[:rows], both[rows:]
    cosines, sines = slice(0, WAVES), slice(WAVES, 2 * WAVES)
    if sines_first:
        cosines, sines = sines, cosines
    return jnp.concatenate(
        [of_real[:, cosines] + of_imag[:, sines], of_imag[:, cosines] - of_real[:, sines]], axis=1
    )


def by_bin(values):
    tile_row = lax.broadcasted_iota(jnp.int32, (TILE, values.shape[1]), 0)
    tiles = [values[at * TILE : (at + 1) * TILE] for at in range(4)]
    four = tiles[2] + pltpu.roll(tiles[2], 4, 0)
    one = pltpu.roll(tiles[3] + pltpu.roll(tiles[3], 7, 0), 4, 0)
    rest = jnp.where(tile_row < 4, four, jnp.where(tile_row == 4, one, 0.0))
    return jnp.concatenate([tiles[0] + tiles[1], rest], axis=0)


def own_kernel(recv_ref, table_ref, cross_ref, real_ref, imag_ref, waves_ref):
    for source in range(DESTS):
        rows = slice(source * TAKEN, (source + 1) * TAKEN)
        real_ref[rows], imag_ref[rows] = parts_of(recv_ref[source])
    waves_ref[...] = spectrum(real_ref[...], imag_ref[...], table_ref[...])
    for half in range(2):
        real_at = half * OFFS
        imag_at = WAVES + half * OFFS

        def body(step, total, real_at=real_at, imag_at=imag_at, half=half):
            row = pl.multiple_of(step * TAKEN, TAKEN)
            total_real, total_imag = total
            own_real = waves_ref[pl.ds(row, TAKEN), real_at : real_at + OFFS]
            own_imag = waves_ref[pl.ds(row, TAKEN), imag_at : imag_at + OFFS]
            for block in range(SEG_BLOCKS):
                if block == SEG_BLOCKS - 1:
                    total_real = total_real + (own_real * own_real + own_imag * own_imag)
                    continue
                at = row + (block + 1) * GROUP
                next_real = waves_ref[pl.ds(at, TAKEN), real_at : real_at + OFFS]
                next_imag = waves_ref[pl.ds(at, TAKEN), imag_at : imag_at + OFFS]
                if half == 0:
                    ext_real, ext_imag = own_real + next_real, own_imag + next_imag
                else:
                    ext_real, ext_imag = own_real - next_real, own_imag - next_imag
                total_real = total_real + (own_real * ext_real + own_imag * ext_imag)
                total_imag = total_imag + (own_imag * ext_real - own_real * ext_imag)
                own_real, own_imag = next_real, next_imag
            return total_real, total_imag

        zero = jnp.zeros((TAKEN, OFFS), F32)
        total = lax.fori_loop(0, WIN_DEVICES, body, (zero, zero))
        cross_ref[:, real_at : real_at + OFFS] = total[0]
        cross_ref[:, imag_at : imag_at + OFFS] = total[1]


def own_products(received, table):
    return pl.pallas_call(
        own_kernel,
        out_shape=jax.ShapeDtypeStruct((TAKEN, 2 * WAVES), F32),
        in_specs=[pl.BlockSpec(memory_space=pltpu.VMEM)] * 2,
        out_specs=pl.BlockSpec(memory_space=pltpu.VMEM),
        scratch_shapes=[
            pltpu.VMEM((DESTS * TAKEN, OFFS), BF16),
            pltpu.VMEM((DESTS * TAKEN, OFFS), BF16),
            pltpu.VMEM((DESTS * TAKEN, 2 * WAVES), F32),
        ],
        compiler_params=pltpu.CompilerParams(vmem_limit_bytes=40 << 20),
        cost_estimate=pl.CostEstimate(
            flops=2 * 1024 * 512 * 1024, bytes_accessed=8 << 20, transcendentals=0
        ),
        name="own_products",
    )(received, table)


def image_kernel(
    ahead_ref, behind_ref, last_ref, table_ref, cross_ref, lead_ref, spread_ref, turns_ref, out_ref
):
    totals = [
        cross_ref[:, at * OFFS : (at + 1) * OFFS] for at in range(4)
    ]
    following = ahead_ref[...] + behind_ref[...]
    slots = [following[w] for w in range(WIN_DEVICES)] + [last_ref[w] for w in range(WIN_DEVICES)]
    reals, imags = zip(*[parts_of(slot) for slot in slots])
    waves = spectrum(
        jnp.concatenate(reals, axis=0), jnp.concatenate(imags, axis=0), table_ref[...], True
    )
    last = waves[GROUP:]
    waves = waves[:GROUP]
    for half in range(2):
        real_at = half * OFFS
        imag_at = WAVES + half * OFFS
        next_real = waves[:, real_at : real_at + OFFS]
        next_imag = waves[:, imag_at : imag_at + OFFS]
        own_real = last[:, real_at : real_at + OFFS]
        own_imag = last[:, imag_at : imag_at + OFFS]
        more_real = own_real * next_real + own_imag * next_imag
        more_imag = own_imag * next_real - own_real * next_imag
        more_real = jnp.sum(more_real.reshape(WIN_DEVICES, TAKEN, OFFS), axis=0)
        more_imag = jnp.sum(more_imag.reshape(WIN_DEVICES, TAKEN, OFFS), axis=0)
        sign = 1.0 if half == 0 else -1.0
        totals[half] = totals[half] + sign * more_real
        totals[2 + half] = totals[2 + half] + sign * more_imag
    cross = by_bin(jnp.concatenate(totals, axis=1))
    flat_real = jnp.sum(cross[:, :WAVES], axis=1, keepdims=True) / WAVES
    flat_imag = jnp.sum(cross[:, WAVES:], axis=1, keepdims=True) / WAVES
    cross = jnp.concatenate([cross[:, :WAVES] - flat_real, cross[:, WAVES:] - flat_imag], axis=0)
    upper = cross.astype(BF16)
    lower = (cross - upper.astype(F32)).astype(BF16)
    both = jnp.dot(
        jnp.concatenate([upper, lower], axis=0), lead_ref[...], preferred_element_type=F32
    )
    both = both[: 2 * SLOT] + both[2 * SLOT :]
    of_real, of_imag = both[:SLOT], both[SLOT:]
    lag = lax.broadcasted_iota(jnp.int32, (SLOT, OFFS), 1)
    real = of_real[:, :OFFS] + of_imag[:, OFFS:] + jnp.where(lag == 0, flat_real, 0.0)
    imag = of_imag[:, :OFFS] - of_real[:, OFFS:] + jnp.where(lag == 0, flat_imag, 0.0)
    power = jnp.sum(real * real + imag * imag, axis=1, keepdims=True) / OFFS
    factor = 1.0 / jnp.sqrt(power + EPS)
    size = SLOT * DIGIT
    row = lax.broadcasted_iota(jnp.int32, (size, OFFS), 0)
    lane = lax.broadcasted_iota(jnp.int32, (size, OFFS), 1)
    same_digit = row // SLOT == lane // DIGIT
    same_bin = row % SLOT == lane % SLOT

    def repeated(values):
        normed = values * factor
        return jnp.broadcast_to(normed[None], (DIGIT, SLOT, OFFS)).reshape(size, OFFS)

    picked = jnp.concatenate(
        [jnp.where(same_digit, repeated(part), 0.0).astype(BF16) for part in (real, imag)], axis=0
    )
    moved = jnp.dot(picked, spread_ref[...], preferred_element_type=F32)
    moved = jnp.concatenate(
        [jnp.where(same_bin, moved[at * size : (at + 1) * size], 0.0) for at in range(2)], axis=0
    ).astype(BF16)
    turns = turns_ref[...]
    fine = [jnp.concatenate(pair, axis=1).astype(BF16) for pair in powers_of(*turn_waves(turns))]
    of_both = jnp.dot(
        moved, jnp.concatenate(fine, axis=0), preferred_element_type=F32
    )
    along = jnp.zeros((SLOT, VEL), F32)
    across = jnp.zeros((SLOT, VEL), F32)
    for at, (cosine, sine) in enumerate(powers_of(*turn_waves(turns * DIGIT))):
        one = of_both[at * SLOT : (at + 1) * SLOT]
        two = of_both[size + at * SLOT : size + (at + 1) * SLOT]
        part_real = one[:, :VEL] + two[:, VEL:]
        part_imag = two[:, :VEL] - one[:, VEL:]
        along = along + (part_real * cosine + part_imag * sine)
        across = across + (part_imag * cosine - part_real * sine)
    image = (along * along + across * across) / OFFS
    here = VEL // SEG_BLOCKS
    for block in range(SEG_BLOCKS):
        pair = image[:, block // 2 * LANES : (block // 2 + 1) * LANES]
        out_ref[block] = pair if block % 2 == 0 else jnp.roll(pair, here, axis=1)


def image_of(*arrays):
    return pl.pallas_call(
        image_kernel,
        out_shape=jax.ShapeDtypeStruct((SEG_BLOCKS, SLOT, LANES), F32),
        in_specs=[pl.BlockSpec(memory_space=pltpu.VMEM)] * 8,
        out_specs=pl.BlockSpec(memory_space=pltpu.VMEM),
        compiler_params=pltpu.CompilerParams(vmem_limit_bytes=40 << 20),
        cost_estimate=pl.CostEstimate(
            flops=2 * 700 * 512 * 1024, bytes_accessed=6 << 20, transcendentals=0
        ),
        name="image",
    )(*arrays)


def gather(parts, table):
    rows = parts.reshape(SEG_BLOCKS * SLOT, LANES)
    gathered = lax.dot_general(
        rows,
        table,
        (((0,), (0,)), ((), ())),
        precision=lax.Precision.HIGHEST,
        preferred_element_type=F32,
    )
    return gathered[: VEL // SEG_BLOCKS]


def local(samples_data, coupling):
    whitened = whiten(samples_data, coupling[None, :], jnp.asarray(time_table()))
    segments = lax.axis_size("seg")
    middle = segments // 2
    place = (lax.axis_index("blk"), lax.axis_index("win"))
    table = jnp.asarray(forward_table())

    def exchange(values):
        return lax.all_to_all(values, ("blk", "win"), 0, 0, tiled=True)

    before = lax.axis_index("seg") < middle
    received = lax.cond(before, lambda values: values, exchange, whitened)
    behind = lax.ppermute(
        received[:WIN_DEVICES], "seg", [(s, s - 1) for s in range(middle, segments)]
    )
    nothing = lax.optimization_barrier(jnp.zeros((TAKEN, 2 * WAVES), F32))
    received, cross, table = lax.cond(
        before,
        lambda values, same, table: (exchange(values), same, table),
        lambda values, _, table: (values, own_products(values, table), table),
        received,
        nothing,
        table,
    )
    behind, received, cross, table = lax.optimization_barrier((behind, received, cross, table))
    ahead = lax.ppermute(received[:WIN_DEVICES], "seg", [(s, s - 1) for s in range(1, middle)])
    cross = lax.cond(
        before,
        lambda values, _, table: own_products(values, table),
        lambda _, same, table: same,
        received,
        cross,
        table,
    )
    images = image_of(
        ahead,
        behind,
        received[-WIN_DEVICES:],
        jnp.asarray(forward_table(sines_first=True)),
        cross,
        jnp.asarray(inverse_table()),
        jnp.asarray(spread_table()),
        turns_of(*place),
    )
    images = lax.all_to_all(images, "blk", 0, 0, tiled=True)
    return gather(images, jnp.asarray(gather_table()))


def solution(mesh):
    segments = mesh.shape["fibre"] // SEG_BLOCKS
    inner = Mesh(
        mesh.devices.reshape(segments, SEG_BLOCKS, mesh.shape["win"]), ("seg", "blk", "win")
    )
    placed = (P("win", None, ("seg", "blk")), P(("seg", "blk")))
    return jax.shard_map(
        local, mesh=inner, in_specs=placed, out_specs=P(("seg", "blk"), "win"), check_vma=False
    )
```
